256 devices in a mesh: ha: 8 (over y, core), wa: 32 (over z, x).
Axes of the slice: x: 4, y: 4, z: 8, core: 2. Of those that a mesh axis runs over, the one named last changes fastest.
Arguments:
- features: bfloat16 [16, 16, 320, 512], P(None, 'ha', 'wa'), may hold values from -90 to 90
- first_cache: bfloat16 [2, 16, 320, 512], P(None, 'ha', 'wa'), may hold values from -6 to 6
- first_gain: float32 [512], replicated, may hold values from 0.1 to 1.9
- first_shift: float32 [512], replicated, may hold values from -3 to 3
- first_weight: bfloat16 [3, 3, 3, 512, 256], replicated, may hold values from -0.0546875 to 0.0546875
- second_cache: bfloat16 [2, 16, 320, 256], P(None, 'ha', 'wa'), may hold values from -6 to 6
- second_gain: float32 [256], replicated, may hold values from 0.1 to 1.9
- second_shift: float32 [256], replicated, may hold values from -3 to 3
- second_weight: bfloat16 [3, 3, 3, 256, 256], replicated, may hold values from -0.078125 to 0.078125
- second_bias: float32 [256], replicated, may hold values from -3 to 3
- skip_weight: bfloat16 [512, 256], replicated, may hold values from -0.0625 to 0.0625
Outputs:
- decoded: bfloat16 [16, 16, 320, 256], P(None, 'ha', 'wa')
The draws below stay inside these ranges and needn't reach their ends.
All inputs are finite; a program needn't handle non-finite values.
Results may differ from the reference program's by a relative error of at most 0.007.
Values may be sent and summed in bfloat16 or wider, within the bound.
A program may use at most 128 MiB of HBM per device.

```python
import jax
import jax.numpy as jnp
from jax import lax

CI = 512
CO = 256
GROUPS = 32
FRAMES = 16
ROWS = 16
COLS = 320


def draw_features(key, part):
    key = jax.random.fold_in(key, 1)
    subkeys = jax.random.split(key, 3)
    shape = (FRAMES, ROWS, COLS, CI)
    row_pos = (jnp.arange(ROWS, dtype=jnp.float32) + 0.5) / ROWS
    col_pos = (jnp.arange(COLS, dtype=jnp.float32) + 0.5) / COLS
    ramp = 10.0 ** (0.5 * row_pos[:, None] + 0.5 * col_pos[None, :])
    cell_scale = jax.random.uniform(subkeys[1], (1, ROWS, COLS, 1), jnp.float32, 0.7, 1.4)
    chan_scale = jax.random.uniform(subkeys[2], (CI,), jnp.float32, 0.6, 1.6)
    noise = jnp.clip(jax.random.normal(subkeys[0], shape, jnp.float32), -4.0, 4.0)
    return (noise * ramp[None, :, :, None] * cell_scale * chan_scale).astype(jnp.bfloat16)


def block_scale(own_key, extent, pieces, low, largest):
    level = 1.0
    for dim, shards_of in pieces:
        steps = jax.random.uniform(jax.random.fold_in(jax.random.fold_in(own_key, 6), dim), (shards_of,), jnp.float32, low / len(pieces), largest / len(pieces))
        level = level * jnp.repeat(jnp.exp(steps), extent[dim] // shards_of).reshape((-1,) + (1,) * (len(extent) - 1 - dim))
    return level


def bell_draw(own_key, dims, deviation, bound, shards=(), kind=jnp.bfloat16):
    values = deviation * jax.random.normal(own_key, dims, jnp.float32)
    if shards:
        values = values * block_scale(own_key, dims, shards, -0.22, 0.18)
    return jnp.clip(values, -bound, bound).astype(kind)


def setup_inputs(seed: int = 0) -> dict:
    seeds = jax.random.split(jax.random.key(seed), 12)
    features = draw_features(jax.random.fold_in(seeds[11], 71), 0)
    first_cache = bell_draw(seeds[1], (2, ROWS, COLS, CI), 1.0, 6.0, ((1, 8), (2, 32)))
    first_gain = jnp.clip(1.0 + 0.18 * jax.random.normal(seeds[2], (CI,), jnp.float32), 0.1, 1.9)
    first_shift = bell_draw(seeds[3], (CI,), 0.5, 3.0, (), jnp.float32)
    first_weight = bell_draw(seeds[4], (3, 3, 3, CI, CO), (27 * CI) ** -0.5, 0.0546875)
    second_cache = bell_draw(seeds[5], (2, ROWS, COLS, CO), 1.0, 6.0, ((1, 8), (2, 32)))
    second_gain = jnp.clip(1.0 + 0.18 * jax.random.normal(seeds[6], (CO,), jnp.float32), 0.1, 1.9)
    second_shift = bell_draw(seeds[7], (CO,), 0.5, 3.0, (), jnp.float32)
    second_weight = bell_draw(seeds[8], (3, 3, 3, CO, CO), (27 * CO) ** -0.5, 0.078125)
    second_bias = bell_draw(seeds[9], (CO,), 0.5, 3.0, (), jnp.float32)
    skip_weight = bell_draw(seeds[10], (CI, CO), (16 * CI) ** -0.5, 0.0625)
    return dict(features=features, first_cache=first_cache, first_gain=first_gain, first_shift=first_shift, first_weight=first_weight, second_cache=second_cache, second_gain=second_gain, second_shift=second_shift, second_weight=second_weight, second_bias=second_bias, skip_weight=skip_weight)


EPSILON = 1e-06

def group_norm(block, gain, shift):
    frames, rows, cols, channels = block.shape
    grouped = block.reshape(frames, rows, cols, GROUPS, channels // GROUPS)
    center = lax.optimization_barrier(jnp.mean(grouped, axis=(0, 1, 2, 4)))
    spread = lax.optimization_barrier(jnp.mean((grouped - center[:, None]) ** 2, axis=(0, 1, 2, 4)))
    normed = (grouped - center[:, None]) * lax.rsqrt(spread + EPSILON)[:, None]
    return normed.reshape(frames, rows, cols, channels) * gain + shift

def causal_conv(padded, weight):
    result = lax.conv_general_dilated(padded.astype(jnp.float32)[None], weight.astype(jnp.float32), (1, 1, 1), ((0, 0), (1, 1), (1, 1)), dimension_numbers=('NDHWC', 'DHWIO', 'NDHWC'), precision=lax.Precision.HIGHEST)
    return result[0]

def reference(features, first_cache, first_gain, first_shift, first_weight, second_cache, second_gain, second_shift, second_weight, second_bias, skip_weight):
    act_one = jax.nn.silu(group_norm(features.astype(jnp.float32), first_gain, first_shift)).astype(jnp.bfloat16)
    middle = causal_conv(jnp.concatenate([first_cache, act_one], axis=0), first_weight).astype(jnp.bfloat16)
    act_two = jax.nn.silu(group_norm(middle.astype(jnp.float32), second_gain, second_shift)).astype(jnp.bfloat16)
    branch = causal_conv(jnp.concatenate([second_cache, act_two], axis=0), second_weight)
    flat = features.reshape(-1, CI)
    skipped = jnp.dot(flat, skip_weight, preferred_element_type=jnp.float32).reshape(FRAMES, ROWS, COLS, CO)
    return (branch + second_bias + skipped).astype(jnp.bfloat16)
```

```python
import functools

import jax
import jax.numpy as jnp
from jax import lax
from jax.experimental import pallas as pl
from jax.experimental.pallas import tpu as pltpu
from jax.sharding import PartitionSpec as P

F32 = jnp.float32
BF16 = jnp.bfloat16
MESH = pl.DeviceIdType.MESH
EPSILON = 1e-06

FRAMES = 16
ROWS, COLS = 2, 10
HALO_ROWS, HALO_COLS = ROWS + 2, COLS + 2
CELLS = ROWS * COLS
CI, CO = 512, 256
GROUPS = 32
NH, NX, NZ = 8, 4, 8
LOCAL = FRAMES * CELLS
DEVICES = NH * NX * NZ

STAGES = (
    tuple((a, b, 0) for a in range(NH) for b in range(NX) if (a, b) != (0, 0)),
    tuple((0, 0, c) for c in range(1, NZ)),
)
SIDES = tuple((a, b) for a in (-1, 0, 1) for b in (-1, 0, 1) if (a, b) != (0, 0))


def place():
    across = lax.axis_index("wa")
    return lax.axis_index("ha"), lax.rem(across, NX), lax.div(across, NX)


def partner(offset):
    row, x, z = place()
    return (
        lax.rem(row + offset[0], NH),
        lax.rem(z + offset[2], NZ) * NX + lax.rem(x + offset[1], NX),
    )


def neighbour(side):
    row, across = lax.axis_index("ha"), lax.axis_index("wa")
    return lax.rem(row + side[0] + NH, NH), lax.rem(across + side[1] + NX * NZ, NX * NZ)


def span(step, extent):
    if step == 0:
        return pl.ds(1, extent), pl.ds(1, extent)
    if step < 0:
        return pl.ds(1, 1), pl.ds(extent + 1, 1)
    return pl.ds(extent, 1), pl.ds(0, 1)


def halo_copy(ref, number, send, recv):
    side = SIDES[number]
    row_from, row_to = span(side[0], ROWS)
    col_from, col_to = span(side[1], COLS)
    return pltpu.make_async_remote_copy(
        src_ref=ref.at[row_from, col_from],
        dst_ref=ref.at[row_to, col_to],
        send_sem=send.at[number],
        recv_sem=recv.at[number],
        device_id=neighbour(side),
        device_id_type=MESH,
    )


def cache_copy(rows_ref, edge_ref, got_rows, got_edge, number, send, recv):
    down, right = SIDES[number]
    if right == 0:
        src = rows_ref.at[0 if down < 0 else 1]
        dst = got_rows.at[1 if down < 0 else 0]
    else:
        src = edge_ref.at[0 if right < 0 else 1]
        dst = got_edge.at[down + 1, 1 if right < 0 else 0]
    return pltpu.make_async_remote_copy(
        src_ref=src,
        dst_ref=dst,
        send_sem=send.at[number],
        recv_sem=recv.at[number],
        device_id=neighbour(SIDES[number]),
        device_id_type=MESH,
    )


def send_stats(stage, src, slots, send, recv):
    for number, offset in enumerate(STAGES[stage]):
        pltpu.make_async_remote_copy(
            src_ref=src,
            dst_ref=slots.at[number],
            send_sem=send,
            recv_sem=recv,
            device_id=partner(offset),
            device_id_type=MESH,
        ).start()


def wait_all(slots, sem):
    pltpu.make_async_copy(slots, slots, sem).wait()


def merge_stats(src, slots, entries):
    tiles = src.shape[0] // 2
    count = slots.shape[0] + 1
    center = (src[:tiles] + jnp.sum(slots[:, :tiles], axis=0)) / count
    off = src[:tiles] - center
    offs = slots[:, :tiles] - center[None]
    spread = src[tiles:] + jnp.sum(slots[:, tiles:], axis=0)
    return center, spread + entries * (off * off + jnp.sum(offs * offs, axis=0))


def as_tiles(row):
    return jnp.concatenate(
        [row[:, 128 * q : 128 * q + 128] for q in range(row.shape[1] // 128)], axis=0
    )


def as_row(tiles):
    return jnp.concatenate([tiles[q : q + 1] for q in range(tiles.shape[0])], axis=1)


def group_stats(center, spread, per_group):
    first = lax.div(lax.broadcasted_iota(jnp.int32, (128, 128), 0), per_group)
    second = lax.div(lax.broadcasted_iota(jnp.int32, (128, 128), 1), per_group)
    same = jnp.where(first == second, 1.0 / per_group, 0.0).astype(F32)
    mean = jnp.dot(center, same, precision=lax.Precision.HIGHEST, preferred_element_type=F32)
    off = center - mean
    each = spread * (1.0 / (LOCAL * DEVICES)) + off * off
    variance = jnp.dot(each, same, precision=lax.Precision.HIGHEST, preferred_element_type=F32)
    return mean, variance


def local_stats(ref, src):
    channels = ref.shape[-1]

    def add(n, total):
        return total + ref[1 + n // COLS, 1 + n % COLS].astype(F32)

    total = lax.fori_loop(0, CELLS, add, jnp.zeros((FRAMES, channels), F32))
    center = jnp.sum(total, axis=0, keepdims=True) / LOCAL

    def add_square(n, total):
        off = ref[1 + n // COLS, 1 + n % COLS].astype(F32) - center
        return total + off * off

    total = lax.fori_loop(0, CELLS, add_square, jnp.zeros((FRAMES, channels), F32))
    spread = jnp.sum(total, axis=0, keepdims=True)
    src[...] = jnp.concatenate([as_tiles(center), as_tiles(spread)], axis=0)


def activate(raw, act, mean, variance, gain, shift):
    row, across = lax.axis_index("ha"), lax.axis_index("wa")
    scale = as_row(lax.rsqrt(variance + EPSILON) * gain * 0.5)
    offset = as_row(shift * 0.5)
    center = as_row(mean)
    for r in range(HALO_ROWS):
        for c in range(HALO_COLS):
            half = (raw[r, c].astype(F32) - center) * scale + offset
            value = half + half * jnp.tanh(half)
            inside = None
            for at, low, high, index, count in (
                (r, 0, HALO_ROWS - 1, row, NH),
                (c, 0, HALO_COLS - 1, across, NX * NZ),
            ):
                if at in (low, high):
                    here = index > 0 if at == low else index < count - 1
                    inside = here if inside is None else jnp.logical_and(inside, here)
            if inside is not None:
                value = jnp.where(inside, value, 0.0)
            act[r, c] = value.astype(BF16)


def convolve(act, weight, first, delayed):
    channels = act.shape[-1]
    result = first
    for time_off in (0, 1, 2):
        total = None
        for row_off in range(3):
            for col_off in range(3):
                window = act[row_off : row_off + ROWS, col_off : col_off + COLS]
                product = jnp.dot(
                    window.reshape(LOCAL, channels),
                    weight[time_off, row_off, col_off],
                    preferred_element_type=F32,
                )
                total = product if total is None else total + product
        late = 2 - time_off
        total = total.reshape(CELLS, FRAMES, CO)
        if late:
            delayed[late - 1, :, 8:, :] = total
            total = delayed[late - 1, :, 8 - late : 8 - late + FRAMES, :]
        result = result + total
    return result


def stage_cache(cache, rows_ref, edge_ref, edge_wide):
    edge_wide[...] = jnp.zeros_like(edge_wide)
    rows_ref[...] = jnp.zeros_like(rows_ref)
    for frame in range(2):
        for r in range(ROWS):
            own = cache[frame, r].astype(F32)
            edge_wide[0, frame * ROWS + r, :] = own[0]
            edge_wide[1, frame * ROWS + r, :] = own[COLS - 1]
            rows_ref[r, frame, 0:COLS, :] = cache[frame, r]
    edge_ref[...] = edge_wide[...].astype(BF16)


def shift_cache(cache, got_rows, got_edge, wide, shifted):
    row, across = lax.axis_index("ha"), lax.axis_index("wa")
    wide[...] = jnp.zeros_like(wide)
    for frame in range(2):
        for r in range(HALO_ROWS):
            inside = {0: row > 0, HALO_ROWS - 1: row < NH - 1}.get(r)
            if inside is None:
                own = cache[frame, r - 1].astype(F32)
                source, entry = 1, frame * ROWS + r - 1
            else:
                upper = r == 0
                own = got_rows[0 if upper else 1, frame].astype(F32)[0:COLS]
                own = jnp.where(inside, own, 0.0)
                source, entry = (2, frame * ROWS + ROWS - 1) if upper else (0, frame * ROWS)
            wide[frame, r, 1 : COLS + 1, :] = own
            for slot, at, here in ((0, 0, across > 0), (1, COLS + 1, across < NX * NZ - 1)):
                edge = got_edge[source, slot].astype(F32)[entry : entry + 1]
                ok = here if inside is None else jnp.logical_and(here, inside)
                wide[frame, r, at : at + 1, :] = jnp.where(ok, edge, 0.0)
    for k in range(3):
        for frame in range(2):
            for r in range(HALO_ROWS):
                shifted[k, frame, r] = wide[frame, r, k : k + 16, :].astype(BF16)


def convolve_cache(shifted, weight, spill):
    channels = shifted.shape[-1]
    both, later = None, None
    for row_off in range(3):
        for k in range(3):
            two = shifted[k, :, row_off : row_off + ROWS].reshape(2 * ROWS * 16, channels)
            one = shifted[k, 1, row_off : row_off + ROWS].reshape(ROWS * 16, channels)
            a = jnp.dot(two, weight[0, row_off, k], preferred_element_type=F32)
            b = jnp.dot(one, weight[1, row_off, k], preferred_element_type=F32)
            both = a if both is None else both + a
            later = b if later is None else later + b
    half = ROWS * 16
    spill[...] = jnp.zeros_like(spill)
    for q in range(CO // 128):
        lanes = slice(128 * q, 128 * q + 128)
        spill[q, 0:half] = both[0:half, lanes] + later[:, lanes]
        spill[q, half : 2 * half] = both[half:, lanes]


def add_cache(spill, total):
    for r in range(ROWS):
        for c in range(COLS):
            for q in range(CO // 128):
                lanes = slice(128 * q, 128 * q + 128)
                total[r * COLS + c, 0:8, lanes] += spill[
                    q, pl.ds(r * 16 + c, 8, stride=ROWS * 16)
                ]


def kernel(
    features, cache_one, gain_one, shift_one, weight_one, cache_two, gain_two, shift_two, weight_two, bias, skip,
    out,
    feats, wide_feats, cells_one, act_one, cells_two, act_two, w_one, w_two, w_skip,
    c_one, c_two, edge_wide_one, edge_wide_two, rows_one, rows_two, edge_one, edge_two,
    got_rows_one, got_rows_two, got_edge_one, got_edge_two,
    wide_one, wide_two, shifted_one, shifted_two, spill, base_one, base_two, delayed,
    src_1a, src_1b, src_2a, src_2b, slots_1a, slots_1b, slots_2a, slots_2b,
    load, stat_send, stat_recv, halo_send, halo_recv,
):
    loads = [
        pltpu.make_async_copy(features, feats, load.at[0]),
        pltpu.make_async_copy(cache_one, c_one, load.at[1]),
        pltpu.make_async_copy(cache_two, c_two, load.at[2]),
        pltpu.make_async_copy(skip, w_skip, load.at[3]),
    ]
    loads += [
        pltpu.make_async_copy(weight_one.at[i], w_one.at[i], load.at[4 + i]) for i in range(3)
    ]
    loads += [
        pltpu.make_async_copy(weight_two.at[i], w_two.at[i], load.at[7 + i]) for i in range(3)
    ]
    for copy in loads:
        copy.start()

    barrier = pltpu.get_barrier_semaphore()
    greeted = [partner(offset) for stage in STAGES for offset in stage]
    greeted += [neighbour(side) for side in SIDES if side[1] != 0]
    for device in greeted:
        pl.semaphore_signal(barrier, inc=1, device_id=device, device_id_type=MESH)

    loads[0].wait()
    for t in range(FRAMES):
        for r in range(ROWS):
            at = (t * ROWS + r) * 16
            for q in range(CI // 128):
                wide_feats[q, at : at + COLS, :] = feats[t, r, :, 128 * q : 128 * q + 128].astype(F32)
    for r in range(ROWS):
        for c in range(COLS):
            for q in range(CI // 128):
                lanes = slice(128 * q, 128 * q + 128)
                cells_one[1 + r, 1 + c, :, lanes] = wide_feats[
                    q, pl.ds(r * 16 + c, FRAMES, stride=ROWS * 16)
                ].astype(BF16)
    local_stats(cells_one, src_1a)
    loads[1].wait()
    loads[2].wait()
    stage_cache(c_one, rows_one, edge_one, edge_wide_one)
    stage_cache(c_two, rows_two, edge_two, edge_wide_two)

    pl.semaphore_wait(barrier, len(greeted))

    send_stats(0, src_1a, slots_1a, stat_send.at[0], stat_recv.at[0])
    halo_one = [halo_copy(cells_one, n, halo_send.at[0], halo_recv.at[0]) for n in range(8)]
    cached_one = [
        cache_copy(rows_one, edge_one, got_rows_one, got_edge_one, n, halo_send.at[1], halo_recv.at[1])
        for n in range(8)
    ]
    cached_two = [
        cache_copy(rows_two, edge_two, got_rows_two, got_edge_two, n, halo_send.at[2], halo_recv.at[2])
        for n in range(8)
    ]
    for copy in halo_one + cached_one + cached_two:
        copy.start()

    loads[3].wait()
    own = cells_one[1 : 1 + ROWS, 1 : 1 + COLS].reshape(LOCAL, CI)
    shortcut = jnp.dot(own, w_skip[...], preferred_element_type=F32) + as_row(bias[...])
    base_two[...] = shortcut.reshape(CELLS, FRAMES, CO)

    wait_all(slots_1a, stat_recv.at[0])
    center, spread = merge_stats(src_1a, slots_1a, LOCAL)
    src_1b[...] = jnp.concatenate([center, spread], axis=0)
    send_stats(1, src_1b, slots_1b, stat_send.at[1], stat_recv.at[1])

    for copy in cached_one:
        copy.wait_recv()
    for n in (4, 5):
        loads[n].wait()
    shift_cache(c_one, got_rows_one, got_edge_one, wide_one, shifted_one)
    convolve_cache(shifted_one, w_one, spill)
    base_one[...] = jnp.zeros_like(base_one)
    add_cache(spill, base_one)

    loads[6].wait()
    delayed[:, :, 0:8, :] = jnp.zeros_like(delayed[:, :, 0:8, :])
    for copy in halo_one:
        copy.wait_recv()
    wait_all(slots_1b, stat_recv.at[1])
    center, spread = merge_stats(src_1b, slots_1b, LOCAL * len(STAGES[0]) + LOCAL)
    mean, variance = group_stats(center, spread, CI // GROUPS)
    activate(cells_one, act_one, mean, variance, gain_one[...], shift_one[...])

    middle = convolve(act_one, w_one, base_one[...], delayed).astype(BF16)
    cells_two[1 : 1 + ROWS, 1 : 1 + COLS] = middle.reshape(ROWS, COLS, FRAMES, CO)
    local_stats(cells_two, src_2a)
    send_stats(0, src_2a, slots_2a, stat_send.at[2], stat_recv.at[2])
    halo_two = [halo_copy(cells_two, n, halo_send.at[3], halo_recv.at[3]) for n in range(8)]
    for copy in halo_two:
        copy.start()

    for copy in cached_two:
        copy.wait_recv()
    for n in (7, 8):
        loads[n].wait()
    shift_cache(c_two, got_rows_two, got_edge_two, wide_two, shifted_two)
    convolve_cache(shifted_two, w_two, spill)
    add_cache(spill, base_two)

    wait_all(slots_2a, stat_recv.at[2])
    center, spread = merge_stats(src_2a, slots_2a, LOCAL)
    src_2b[...] = jnp.concatenate([center, spread], axis=0)
    send_stats(1, src_2b, slots_2b, stat_send.at[3], stat_recv.at[3])

    loads[9].wait()
    for copy in halo_one + cached_one + cached_two + halo_two:
        copy.wait_send()
    wait_all(slots_1a, stat_send.at[0])
    wait_all(slots_1b, stat_send.at[1])
    wait_all(slots_2a, stat_send.at[2])
    for copy in halo_two:
        copy.wait_recv()
    wait_all(slots_2b, stat_recv.at[3])
    center, spread = merge_stats(src_2b, slots_2b, LOCAL * len(STAGES[0]) + LOCAL)
    mean, variance = group_stats(center, spread, CO // GROUPS)
    activate(cells_two, act_two, mean, variance, gain_two[...], shift_two[...])
    decoded = convolve(act_two, w_two, base_two[...], delayed)
    out[...] = decoded.reshape(ROWS, COLS, FRAMES, CO).astype(BF16)
    wait_all(slots_2b, stat_send.at[3])


def on_device(
    features, first_cache, first_gain, first_shift, first_weight,
    second_cache, second_gain, second_shift, second_weight, second_bias, skip_weight,
):
    vmem = pl.BlockSpec(memory_space=pltpu.VMEM)
    hbm = pl.BlockSpec(memory_space=pl.ANY)
    near, far = len(STAGES[0]), len(STAGES[1])
    cells = (HALO_ROWS, HALO_COLS, FRAMES)

    def per_conv(channels):
        return [
            pltpu.VMEM((2, ROWS, COLS, channels), BF16),
            pltpu.VMEM((2, 16, channels), F32),
            pltpu.VMEM((ROWS, 2, 16, channels), BF16),
            pltpu.VMEM((2, 16, channels), BF16),
            pltpu.VMEM((2, 2, 16, channels), BF16),
            pltpu.VMEM((3, 2, 16, channels), BF16),
            pltpu.VMEM((2, HALO_ROWS, 24, channels), F32),
            pltpu.VMEM((3, 2, HALO_ROWS, 16, channels), BF16),
        ]

    one, two = per_conv(CI), per_conv(CO)
    paired = [scratch for pair in zip(one, two) for scratch in pair]
    out = pl.pallas_call(
        kernel,
        out_shape=jax.ShapeDtypeStruct((ROWS, COLS, FRAMES, CO), BF16),
        in_specs=[hbm, hbm, vmem, vmem, hbm, hbm, vmem, vmem, hbm, vmem, hbm],
        out_specs=vmem,
        scratch_shapes=[
            pltpu.VMEM((FRAMES, ROWS, COLS, CI), BF16),
            pltpu.VMEM((CI // 128, FRAMES * ROWS * 16, 128), F32),
            pltpu.VMEM(cells + (CI,), BF16),
            pltpu.VMEM(cells + (CI,), BF16),
            pltpu.VMEM(cells + (CO,), BF16),
            pltpu.VMEM(cells + (CO,), BF16),
            pltpu.VMEM((3, 3, 3, CI, CO), BF16),
            pltpu.VMEM((3, 3, 3, CO, CO), BF16),
            pltpu.VMEM((CI, CO), BF16),
            *paired,
            pltpu.VMEM((CO // 128, 8 * ROWS * 16, 128), F32),
            pltpu.VMEM((CELLS, FRAMES, CO), F32),
            pltpu.VMEM((CELLS, FRAMES, CO), F32),
            pltpu.VMEM((2, CELLS, FRAMES + 8, CO), F32),
            pltpu.VMEM((2 * CI // 128, 128), F32),
            pltpu.VMEM((2 * CI // 128, 128), F32),
            pltpu.VMEM((2 * CO // 128, 128), F32),
            pltpu.VMEM((2 * CO // 128, 128), F32),
            pltpu.VMEM((near, 2 * CI // 128, 128), F32),
            pltpu.VMEM((far, 2 * CI // 128, 128), F32),
            pltpu.VMEM((near, 2 * CO // 128, 128), F32),
            pltpu.VMEM((far, 2 * CO // 128, 128), F32),
            pltpu.SemaphoreType.DMA((10,)),
            pltpu.SemaphoreType.DMA((4,)),
            pltpu.SemaphoreType.DMA((4,)),
            pltpu.SemaphoreType.DMA((4, 8)),
            pltpu.SemaphoreType.DMA((4, 8)),
        ],
        compiler_params=pltpu.CompilerParams(
            collective_id=0, has_side_effects=True, vmem_limit_bytes=48 << 20
        ),
        cost_estimate=pl.CostEstimate(
            flops=2 * LOCAL * CO * (27 * CI + 27 * CO + CI),
            bytes_accessed=2 * (27 * (CI + CO) + CI) * CO + 2 * LOCAL * (CI + CO),
            transcendentals=48 * FRAMES * (CI + CO),
        ),
    )(
        features,
        first_cache,
        first_gain.reshape(CI // 128, 128),
        first_shift.reshape(CI // 128, 128),
        first_weight,
        second_cache,
        second_gain.reshape(CO // 128, 128),
        second_shift.reshape(CO // 128, 128),
        second_weight,
        second_bias.reshape(CO // 128, 128),
        skip_weight,
    )
    return jnp.transpose(out, (2, 0, 1, 3))


def solution(mesh):
    tile = P(None, "ha", "wa", None)
    return jax.shard_map(
        on_device,
        mesh=mesh,
        in_specs=(tile, tile, P(), P(), P(), tile, P(), P(), P(), P(), P()),
        out_specs=tile,
        check_vma=False,
    )
```

```python
import functools

import jax
import jax.numpy as jnp
from jax import lax
from jax.experimental import pallas as pl
from jax.experimental.pallas import tpu as pltpu
from jax.sharding import PartitionSpec as P

F32 = jnp.float32
BF16 = jnp.bfloat16
MESH = pl.DeviceIdType.MESH
EPSILON = 1e-06

FRAMES = 16
ROWS, COLS = 2, 10
HALO_ROWS, HALO_COLS = ROWS + 2, COLS + 2
CELLS = ROWS * COLS
CI, CO = 512, 256
GROUPS = 32
NH, NX, NZ = 8, 4, 8
LOCAL = FRAMES * CELLS
DEVICES = NH * NX * NZ

def hops(offset):
    row, x, z = offset
    return min(row, NH - row) / 2 + min(x, NX - x) + min(z, NZ - z)


STAGES = tuple(
    tuple(sorted(stage, key=lambda offset: -hops(offset)))
    for stage in (
        [(a, b, 0) for a in range(NH) for b in range(NX) if (a, b) != (0, 0)],
        [(0, 0, c) for c in range(1, NZ)],
    )
)
SIDES = tuple((a, b) for a in (-1, 0, 1) for b in (-1, 0, 1) if (a, b) != (0, 0))


def place():
    across = lax.axis_index("wa")
    return lax.axis_index("ha"), lax.rem(across, NX), lax.div(across, NX)


def partner(offset):
    row, x, z = place()
    return (
        lax.rem(row + offset[0], NH),
        lax.rem(z + offset[2], NZ) * NX + lax.rem(x + offset[1], NX),
    )


def neighbour(side):
    row, across = lax.axis_index("ha"), lax.axis_index("wa")
    return lax.rem(row + side[0] + NH, NH), lax.rem(across + side[1] + NX * NZ, NX * NZ)


def span(step, extent):
    if step == 0:
        return pl.ds(1, extent), pl.ds(1, extent)
    if step < 0:
        return pl.ds(1, 1), pl.ds(extent + 1, 1)
    return pl.ds(extent, 1), pl.ds(0, 1)


def halo_copy(ref, number, send, recv):
    side = SIDES[number]
    row_from, row_to = span(side[0], ROWS)
    col_from, col_to = span(side[1], COLS)
    return pltpu.make_async_remote_copy(
        src_ref=ref.at[row_from, col_from],
        dst_ref=ref.at[row_to, col_to],
        send_sem=send.at[number],
        recv_sem=recv.at[number],
        device_id=neighbour(side),
        device_id_type=MESH,
    )


def cache_copy(rows_ref, edge_ref, got_rows, got_edge, number, send, recv):
    down, right = SIDES[number]
    if right == 0:
        src = rows_ref.at[0 if down < 0 else 1]
        dst = got_rows.at[1 if down < 0 else 0]
    else:
        src = edge_ref.at[0 if right < 0 else 1]
        dst = got_edge.at[down + 1, 1 if right < 0 else 0]
    return pltpu.make_async_remote_copy(
        src_ref=src,
        dst_ref=dst,
        send_sem=send.at[number],
        recv_sem=recv.at[number],
        device_id=neighbour(SIDES[number]),
        device_id_type=MESH,
    )


def send_stats(stage, src, slots, send, recv):
    for number, offset in enumerate(STAGES[stage]):
        pltpu.make_async_remote_copy(
            src_ref=src,
            dst_ref=slots.at[number],
            send_sem=send,
            recv_sem=recv,
            device_id=partner(offset),
            device_id_type=MESH,
        ).start()


def wait_all(slots, sem):
    pltpu.make_async_copy(slots, slots, sem).wait()


def merge_stats(src, slots, entries):
    count = slots.shape[0] + 1
    own = src[...]
    others = slots[...]
    total = own + jnp.sum(others, axis=0)
    center = total[0:1] / count
    off = own[0:1] - center
    offs = others[:, 0] - center
    squares = off * off + jnp.sum(offs * offs, axis=0, keepdims=True)
    return center, total[1:2] + entries * squares


def as_tiles(row):
    return jnp.concatenate(
        [row[:, 128 * q : 128 * q + 128] for q in range(row.shape[1] // 128)], axis=0
    )


def as_row(tiles):
    return jnp.concatenate([tiles[q : q + 1] for q in range(tiles.shape[0])], axis=1)


def group_sum(tiles, per_group):
    rows = tiles.shape[0]
    first = lax.div(lax.broadcasted_iota(jnp.int32, (128, 128), 0), per_group)
    second = lax.div(lax.broadcasted_iota(jnp.int32, (128, 128), 1), per_group)
    same = jnp.where(first == second, 1.0, 0.0).astype(BF16)
    if rows < 8:
        tiles = jnp.concatenate([tiles, jnp.zeros((8 - rows, 128), F32)], axis=0)
    high = tiles.astype(BF16).astype(F32)
    rest = tiles - high
    middle = rest.astype(BF16).astype(F32)
    terms = jnp.concatenate([high, middle, rest - middle], axis=0).astype(BF16)
    sums = jnp.dot(terms, same, preferred_element_type=F32)
    return (sums[0:8] + sums[8:16] + sums[16:24])[:rows]


def lane_of(rows, per_group):
    lane = lax.rem(lax.broadcasted_iota(jnp.int32, (rows, 128), 1), per_group)
    return lane == lax.broadcasted_iota(jnp.int32, (rows, 128), 0)


def pack_groups(tiles, per_group):
    mask = lane_of(tiles.shape[0], per_group)
    return jnp.sum(jnp.where(mask, tiles, 0.0), axis=0, keepdims=True)


def unpack_groups(center, spread, rows, per_group):
    mask = lane_of(rows, per_group)
    picked = [jnp.where(mask, jnp.broadcast_to(row, (rows, 128)), 0.0) for row in (center, spread)]
    sums = group_sum(jnp.concatenate(picked, axis=0), per_group)
    return sums[:rows], sums[rows:] * (1.0 / (LOCAL * DEVICES * per_group))


def local_stats(cells, src):
    channels = cells.shape[-1]
    per_group = channels // GROUPS
    center = jnp.sum(cells, axis=0, keepdims=True) * (1.0 / LOCAL)
    off = cells - center
    spread = as_tiles(jnp.sum(off * off, axis=0, keepdims=True))
    center = as_tiles(center)
    mean = group_sum(center, per_group) * (1.0 / per_group)
    off = center - mean
    spread = group_sum(spread + LOCAL * (off * off), per_group)
    src[0:1] = pack_groups(mean, per_group)
    src[1:2] = pack_groups(spread, per_group)


class Activation:
    def __init__(self, raw, act, mean, variance, gain, shift):
        self.raw, self.act = raw, act
        self.center = as_row(mean)
        self.scale = as_row(lax.rsqrt(variance + EPSILON) * gain * 0.5)
        self.offset = as_row(shift * 0.5)

    def cell(self, r, c):
        half = (self.raw[r, c].astype(F32) - self.center) * self.scale + self.offset
        value = half + half * jnp.tanh(half)
        inside = None
        for at, extent, index, count in (
            (r, HALO_ROWS, lax.axis_index("ha"), NH),
            (c, HALO_COLS, lax.axis_index("wa"), NX * NZ),
        ):
            if at in (0, extent - 1):
                here = index > 0 if at == 0 else index < count - 1
                inside = here if inside is None else jnp.logical_and(inside, here)
        if inside is not None:
            value = jnp.where(inside, value, 0.0)
        self.act[r, c] = value.astype(BF16)


TAPS = ((1, 1), (0, 1), (2, 1), (1, 0), (1, 2), (0, 0), (0, 2), (2, 0), (2, 2))


def convolve(activation, weight, first, delayed):
    act = activation.act
    channels = act.shape[-1]
    made = set()
    result = first
    for time_off in range(3):
        total = None
        for row_off, col_off in TAPS:
            for r in range(row_off, row_off + ROWS):
                for c in range(col_off, col_off + COLS):
                    if (r, c) not in made:
                        activation.cell(r, c)
                        made.add((r, c))
            window = act[row_off : row_off + ROWS, col_off : col_off + COLS]
            product = jnp.dot(
                window.reshape(LOCAL, channels),
                weight[time_off, row_off, col_off],
                preferred_element_type=F32,
            )
            total = product if total is None else total + product
        total = total.reshape(CELLS, FRAMES, CO)
        late = 2 - time_off
        if late:
            delayed[late - 1, :, 8:, :] = total
            total = delayed[late - 1, :, 8 - late : 8 - late + FRAMES, :]
        result = result + total
    return result


def stage_cache(cache, wide, rows_ref, edge_ref, edge_wide):
    edge_wide[...] = jnp.zeros_like(edge_wide)
    wide[...] = jnp.zeros_like(wide)
    for frame in range(2):
        for c in range(COLS):
            both = cache[frame, c].astype(F32)
            for r in range(ROWS):
                wide[frame, 1 + r, 1 + c : 2 + c, :] = both[r : r + 1]
            if c in (0, COLS - 1):
                edge_wide[min(c, 1), frame * ROWS : frame * ROWS + ROWS, :] = both
        for r in range(ROWS):
            rows_ref[r, frame] = wide[frame, 1 + r, 1:17, :].astype(BF16)
    edge_ref[...] = edge_wide[...].astype(BF16)


def shift_cache(got_rows, got_edge, wide, shifted):
    row, across = lax.axis_index("ha"), lax.axis_index("wa")
    for frame in range(2):
        for r in range(HALO_ROWS):
            inside = {0: row > 0, HALO_ROWS - 1: row < NH - 1}.get(r)
            if inside is None:
                source, entry = 1, frame * ROWS + r - 1
            else:
                upper = r == 0
                own = got_rows[0 if upper else 1, frame].astype(F32)[0:COLS]
                wide[frame, r, 1 : COLS + 1, :] = jnp.where(inside, own, 0.0)
                source, entry = (2, frame * ROWS + ROWS - 1) if upper else (0, frame * ROWS)
            for slot, at, here in ((0, 0, across > 0), (1, COLS + 1, across < NX * NZ - 1)):
                edge = got_edge[source, slot].astype(F32)[entry : entry + 1]
                ok = here if inside is None else jnp.logical_and(here, inside)
                wide[frame, r, at : at + 1, :] = jnp.where(ok, edge, 0.0)
    for k in range(3):
        for frame in range(2):
            for r in range(HALO_ROWS):
                shifted[k, frame, r] = wide[frame, r, k : k + 16, :].astype(BF16)


def convolve_cache(shifted, weight, spill):
    channels = shifted.shape[-1]
    both, later = None, None
    for row_off in range(3):
        for k in range(3):
            two = shifted[k, :, row_off : row_off + ROWS].reshape(2 * ROWS * 16, channels)
            one = shifted[k, 1, row_off : row_off + ROWS].reshape(ROWS * 16, channels)
            a = jnp.dot(two, weight[0, row_off, k], preferred_element_type=F32)
            b = jnp.dot(one, weight[1, row_off, k], preferred_element_type=F32)
            both = a if both is None else both + a
            later = b if later is None else later + b
    half = ROWS * 16
    spill[...] = jnp.zeros_like(spill)
    for q in range(CO // 128):
        lanes = slice(128 * q, 128 * q + 128)
        spill[q, 0:half] = both[0:half, lanes] + later[:, lanes]
        spill[q, half : 2 * half] = both[half:, lanes]


def add_cache(spill, total):
    for r in range(ROWS):
        for c in range(COLS):
            for q in range(CO // 128):
                lanes = slice(128 * q, 128 * q + 128)
                total[r * COLS + c, 0:8, lanes] += spill[
                    q, pl.ds(r * 16 + c, 8, stride=ROWS * 16)
                ]


def kernel(
    features, cache_one, gain_one_in, shift_one_in, weight_one, cache_two, gain_two_in, shift_two_in, weight_two,
    bias_in, skip,
    out,
    gain_one, shift_one, gain_two, shift_two, bias,
    feats, wide_feats, cells_one, act_one, cells_two, act_two, w_one, w_two, w_skip,
    c_one, c_two, edge_wide_one, edge_wide_two, rows_one, rows_two, edge_one, edge_two,
    got_rows_one, got_rows_two, got_edge_one, got_edge_two,
    wide_one, wide_two, shifted_one, shifted_two, spill, base_one, base_two, delayed,
    src_1a, src_1b, src_2a, src_2b, slots_1a, slots_1b, slots_2a, slots_2b,
    load, stat_send, stat_recv, halo_send, halo_recv,
):
    near = len(STAGES[0])
    loads = [
        pltpu.make_async_copy(features, feats, load.at[0]),
        pltpu.make_async_copy(cache_one, c_one, load.at[1]),
        pltpu.make_async_copy(cache_two, c_two, load.at[2]),
        pltpu.make_async_copy(skip, w_skip, load.at[3]),
    ]
    loads += [
        pltpu.make_async_copy(weight_one.at[i], w_one.at[i], load.at[4 + i]) for i in range(3)
    ]
    loads += [
        pltpu.make_async_copy(weight_two.at[i], w_two.at[i], load.at[7 + i]) for i in range(3)
    ]
    vectors = ((gain_one_in, gain_one), (shift_one_in, shift_one), (gain_two_in, gain_two),
               (shift_two_in, shift_two), (bias_in, bias))
    loads += [pltpu.make_async_copy(*pair, load.at[10 + n]) for n, pair in enumerate(vectors)]
    loads[0].start()

    barrier = pltpu.get_barrier_semaphore()
    greeted = [partner(offset) for stage in STAGES for offset in stage]
    greeted += [neighbour(side) for side in SIDES if side[1] != 0]
    for device in greeted:
        pl.semaphore_signal(barrier, inc=1, device_id=device, device_id_type=MESH)
    for copy in loads[1:]:
        copy.start()

    loads[0].wait()
    for t in range(FRAMES):
        for c in range(COLS):
            at = (t * COLS + c) * ROWS
            both = feats[t, c].astype(F32)
            for q in range(CI // 128):
                wide_feats[q, at : at + ROWS, :] = both[:, 128 * q : 128 * q + 128]
    for r in range(ROWS):
        for c in range(COLS):
            for q in range(CI // 128):
                lanes = slice(128 * q, 128 * q + 128)
                cells_one[1 + r, 1 + c, :, lanes] = wide_feats[
                    q, pl.ds(c * ROWS + r, FRAMES, stride=CELLS)
                ].astype(BF16)
    own = cells_one[1 : 1 + ROWS, 1 : 1 + COLS].reshape(LOCAL, CI)
    local_stats(own.astype(F32), src_1a)
    loads[1].wait()
    loads[2].wait()
    stage_cache(c_one, wide_one, rows_one, edge_one, edge_wide_one)
    stage_cache(c_two, wide_two, rows_two, edge_two, edge_wide_two)

    pl.semaphore_wait(barrier, len(greeted))

    send_stats(0, src_1a, slots_1a, stat_send.at[0], stat_recv.at[0])
    halo_one = [halo_copy(cells_one, n, halo_send.at[0], halo_recv.at[0]) for n in range(8)]
    cached_one = [
        cache_copy(rows_one, edge_one, got_rows_one, got_edge_one, n, halo_send.at[1], halo_recv.at[1])
        for n in range(8)
    ]
    cached_two = [
        cache_copy(rows_two, edge_two, got_rows_two, got_edge_two, n, halo_send.at[2], halo_recv.at[2])
        for n in range(8)
    ]
    for copy in halo_one + cached_one + cached_two:
        copy.start()

    for copy in loads[10:] + loads[3:4]:
        copy.wait()
    own = cells_one[1 : 1 + ROWS, 1 : 1 + COLS].reshape(LOCAL, CI)
    shortcut = jnp.dot(own, w_skip[...], preferred_element_type=F32) + as_row(bias[...])
    base_two[...] = shortcut.reshape(CELLS, FRAMES, CO)

    wait_all(slots_1a, stat_recv.at[0])
    src_1b[0:1], src_1b[1:2] = merge_stats(src_1a, slots_1a, LOCAL * CI // GROUPS)
    send_stats(1, src_1b, slots_1b, stat_send.at[1], stat_recv.at[1])

    for copy in cached_one:
        copy.wait_recv()
    for n in (4, 5):
        loads[n].wait()
    shift_cache(got_rows_one, got_edge_one, wide_one, shifted_one)
    convolve_cache(shifted_one, w_one, spill)
    base_one[...] = jnp.zeros_like(base_one)
    add_cache(spill, base_one)

    loads[6].wait()
    delayed[:, :, 0:8, :] = jnp.zeros_like(delayed[:, :, 0:8, :])
    for copy in halo_one:
        copy.wait_recv()
    wait_all(slots_1b, stat_recv.at[1])
    center, spread = merge_stats(src_1b, slots_1b, LOCAL * (near + 1) * CI // GROUPS)
    mean, variance = unpack_groups(center, spread, CI // 128, CI // GROUPS)
    activation = Activation(cells_one, act_one, mean, variance, gain_one[...], shift_one[...])
    middle = convolve(activation, w_one, base_one[...], delayed).astype(BF16)
    cells_two[1 : 1 + ROWS, 1 : 1 + COLS] = middle.reshape(ROWS, COLS, FRAMES, CO)
    local_stats(middle.astype(F32).reshape(LOCAL, CO), src_2a)
    send_stats(0, src_2a, slots_2a, stat_send.at[2], stat_recv.at[2])
    halo_two = [halo_copy(cells_two, n, halo_send.at[3], halo_recv.at[3]) for n in range(8)]
    for copy in halo_two:
        copy.start()

    for copy in cached_two:
        copy.wait_recv()
    for n in (7, 8):
        loads[n].wait()
    shift_cache(got_rows_two, got_edge_two, wide_two, shifted_two)
    convolve_cache(shifted_two, w_two, spill)
    add_cache(spill, base_two)

    wait_all(slots_2a, stat_recv.at[2])
    src_2b[0:1], src_2b[1:2] = merge_stats(src_2a, slots_2a, LOCAL * CO // GROUPS)
    send_stats(1, src_2b, slots_2b, stat_send.at[3], stat_recv.at[3])

    loads[9].wait()
    for copy in halo_one + cached_one + cached_two + halo_two:
        copy.wait_send()
    wait_all(slots_1a, stat_send.at[0])
    wait_all(slots_1b, stat_send.at[1])
    wait_all(slots_2a, stat_send.at[2])
    for copy in halo_two:
        copy.wait_recv()
    wait_all(slots_2b, stat_recv.at[3])
    center, spread = merge_stats(src_2b, slots_2b, LOCAL * (near + 1) * CO // GROUPS)
    mean, variance = unpack_groups(center, spread, CO // 128, CO // GROUPS)
    activation = Activation(cells_two, act_two, mean, variance, gain_two[...], shift_two[...])
    decoded = convolve(activation, w_two, base_two[...], delayed)
    out[...] = decoded.reshape(ROWS, COLS, FRAMES, CO).astype(BF16)
    wait_all(slots_2b, stat_send.at[3])


def by_column(tile):
    return jnp.transpose(tile, (0, 2, 1, 3))


def on_device(
    features, first_cache, first_gain, first_shift, first_weight,
    second_cache, second_gain, second_shift, second_weight, second_bias, skip_weight,
):
    vmem = pl.BlockSpec(memory_space=pltpu.VMEM)
    hbm = pl.BlockSpec(memory_space=pltpu.HBM)
    near, far = len(STAGES[0]), len(STAGES[1])
    cells = (HALO_ROWS, HALO_COLS, FRAMES)

    def per_conv(channels):
        return [
            pltpu.VMEM((2, COLS, ROWS, channels), BF16),
            pltpu.VMEM((2, 16, channels), F32),
            pltpu.VMEM((ROWS, 2, 16, channels), BF16),
            pltpu.VMEM((2, 16, channels), BF16),
            pltpu.VMEM((2, 2, 16, channels), BF16),
            pltpu.VMEM((3, 2, 16, channels), BF16),
            pltpu.VMEM((2, HALO_ROWS, 24, channels), F32),
            pltpu.VMEM((3, 2, HALO_ROWS, 16, channels), BF16),
        ]

    one, two = per_conv(CI), per_conv(CO)
    paired = [scratch for pair in zip(one, two) for scratch in pair]
    out = pl.pallas_call(
        kernel,
        out_shape=pltpu.VMEM((ROWS, COLS, FRAMES, CO), BF16),
        in_specs=[hbm] * 11,
        out_specs=vmem,
        scratch_shapes=[
            pltpu.VMEM((CI // 128, 128), F32),
            pltpu.VMEM((CI // 128, 128), F32),
            pltpu.VMEM((CO // 128, 128), F32),
            pltpu.VMEM((CO // 128, 128), F32),
            pltpu.VMEM((CO // 128, 128), F32),
            pltpu.VMEM((FRAMES, COLS, ROWS, CI), BF16),
            pltpu.VMEM((CI // 128, LOCAL, 128), F32),
            pltpu.VMEM(cells + (CI,), BF16),
            pltpu.VMEM(cells + (CI,), BF16),
            pltpu.VMEM(cells + (CO,), BF16),
            pltpu.VMEM(cells + (CO,), BF16),
            pltpu.VMEM((3, 3, 3, CI, CO), BF16),
            pltpu.VMEM((3, 3, 3, CO, CO), BF16),
            pltpu.VMEM((CI, CO), BF16),
            *paired,
            pltpu.VMEM((CO // 128, 8 * ROWS * 16, 128), F32),
            pltpu.VMEM((CELLS, FRAMES, CO), F32),
            pltpu.VMEM((CELLS, FRAMES, CO), F32),
            pltpu.VMEM((2, CELLS, FRAMES + 8, CO), F32),
            *[pltpu.VMEM((2, 128), F32) for _ in range(4)],
            *[pltpu.VMEM((count, 2, 128), F32) for _ in range(2) for count in (near, far)],
            pltpu.SemaphoreType.DMA((15,)),
            pltpu.SemaphoreType.DMA((4,)),
            pltpu.SemaphoreType.DMA((4,)),
            pltpu.SemaphoreType.DMA((4, 8)),
            pltpu.SemaphoreType.DMA((4, 8)),
        ],
        compiler_params=pltpu.CompilerParams(
            collective_id=0, has_side_effects=True, vmem_limit_bytes=63 << 20
        ),
        cost_estimate=pl.CostEstimate(
            flops=2 * LOCAL * CO * (27 * CI + 27 * CO + CI),
            bytes_accessed=2 * (27 * (CI + CO) + CI) * CO + 2 * LOCAL * (CI + CO),
            transcendentals=48 * FRAMES * (CI + CO),
        ),
    )(
        by_column(features),
        by_column(first_cache),
        first_gain.reshape(CI // 128, 128),
        first_shift.reshape(CI // 128, 128),
        first_weight,
        by_column(second_cache),
        second_gain.reshape(CO // 128, 128),
        second_shift.reshape(CO // 128, 128),
        second_weight,
        second_bias.reshape(CO // 128, 128),
        skip_weight,
    )
    return jnp.transpose(out, (2, 0, 1, 3))


def solution(mesh):
    tile = P(None, "ha", "wa", None)
    return jax.shard_map(
        on_device,
        mesh=mesh,
        in_specs=(tile, tile, P(), P(), P(), tile, P(), P(), P(), P(), P()),
        out_specs=tile,
        check_vma=False,
    )
```

```python
import functools

import jax
import jax.numpy as jnp
from jax import lax
from jax.experimental import pallas as pl
from jax.experimental.pallas import tpu as pltpu
from jax.sharding import PartitionSpec as P

F32 = jnp.float32
BF16 = jnp.bfloat16
MESH = pl.DeviceIdType.MESH
EPSILON = 1e-06

FRAMES = 16
ROWS, COLS = 2, 10
HALO_ROWS, HALO_COLS = ROWS + 2, COLS + 2
CELLS = ROWS * COLS
CI, CO = 512, 256
GROUPS = 32
NH, NX, NZ = 8, 4, 8
LOCAL = FRAMES * CELLS
DEVICES = NH * NX * NZ

def hops(offset):
    row, x, z = offset
    return min(row, NH - row) / 2 + min(x, NX - x) + min(z, NZ - z)


STAGES = tuple(
    tuple(sorted(stage, key=lambda offset: -hops(offset)))
    for stage in (
        [(0, 0, c) for c in range(1, NZ)],
        [(a, b, 0) for a in range(NH) for b in range(NX) if (a, b) != (0, 0)],
    )
)
DIRECT = tuple(
    sorted(
        (
            (a, b, c)
            for a in range(0, NH, 2)
            for b in range(NX)
            for c in range(NZ)
            if (a, b, c) != (0, 0, 0)
        ),
        key=lambda offset: -hops(offset),
    )
)
FAR = sum(hops(offset) >= 6 for offset in DIRECT)
SIDES = tuple((a, b) for a in (-1, 0, 1) for b in (-1, 0, 1) if (a, b) != (0, 0))


def place():
    across = lax.axis_index("wa")
    return lax.axis_index("ha"), lax.rem(across, NX), lax.div(across, NX)


def partner(offset):
    row, x, z = place()
    return (
        lax.rem(row + offset[0], NH),
        lax.rem(z + offset[2], NZ) * NX + lax.rem(x + offset[1], NX),
    )


def neighbour(side):
    row, across = lax.axis_index("ha"), lax.axis_index("wa")
    return lax.rem(row + side[0] + NH, NH), lax.rem(across + side[1] + NX * NZ, NX * NZ)


def span(step, extent):
    if step == 0:
        return pl.ds(1, extent), pl.ds(1, extent)
    if step < 0:
        return pl.ds(1, 1), pl.ds(extent + 1, 1)
    return pl.ds(extent, 1), pl.ds(0, 1)


def halo_copy(ref, number, send, recv):
    side = SIDES[number]
    row_from, row_to = span(side[0], ROWS)
    col_from, col_to = span(side[1], COLS)
    return pltpu.make_async_remote_copy(
        src_ref=ref.at[row_from, col_from],
        dst_ref=ref.at[row_to, col_to],
        send_sem=send.at[number],
        recv_sem=recv.at[number],
        device_id=neighbour(side),
        device_id_type=MESH,
    )


def cache_copy(rows_ref, edge_ref, got_rows, got_edge, number, send, recv):
    down, right = SIDES[number]
    if right == 0:
        src = rows_ref.at[0 if down < 0 else 1]
        dst = got_rows.at[1 if down < 0 else 0]
    else:
        src = edge_ref.at[0 if right < 0 else 1]
        dst = got_edge.at[down + 1, 1 if right < 0 else 0]
    return pltpu.make_async_remote_copy(
        src_ref=src,
        dst_ref=dst,
        send_sem=send.at[number],
        recv_sem=recv.at[number],
        device_id=neighbour(SIDES[number]),
        device_id_type=MESH,
    )


def send_stats(offsets, src, slots, send, recv, begin=0, end=None):
    for number, offset in list(enumerate(offsets))[begin:end]:
        pltpu.make_async_remote_copy(
            src_ref=src,
            dst_ref=slots.at[number],
            send_sem=send,
            recv_sem=recv,
            device_id=partner(offset),
            device_id_type=MESH,
        ).start()


def wait_all(slots, sem):
    pltpu.make_async_copy(slots, slots, sem).wait()


def merge_stats(src, slots, entries):
    count = slots.shape[0] + 1
    own = src[...]
    others = slots[...]
    total = own + jnp.sum(others, axis=0)
    center = total[0:1] / count
    off = own[0:1] - center
    offs = others[:, 0] - center
    squares = off * off + jnp.sum(offs * offs, axis=0, keepdims=True)
    return center, total[1:2] + entries * squares


def as_tiles(row):
    return jnp.concatenate(
        [row[:, 128 * q : 128 * q + 128] for q in range(row.shape[1] // 128)], axis=0
    )


def as_row(tiles):
    return jnp.concatenate([tiles[q : q + 1] for q in range(tiles.shape[0])], axis=1)


def group_sum(tiles, per_group):
    rows = tiles.shape[0]
    first = lax.div(lax.broadcasted_iota(jnp.int32, (128, 128), 0), per_group)
    second = lax.div(lax.broadcasted_iota(jnp.int32, (128, 128), 1), per_group)
    same = jnp.where(first == second, 1.0, 0.0).astype(BF16)
    if rows < 8:
        tiles = jnp.concatenate([tiles, jnp.zeros((8 - rows, 128), F32)], axis=0)
    high = tiles.astype(BF16).astype(F32)
    rest = tiles - high
    middle = rest.astype(BF16).astype(F32)
    terms = jnp.concatenate([high, middle, rest - middle], axis=0).astype(BF16)
    sums = jnp.dot(terms, same, preferred_element_type=F32)
    return (sums[0:8] + sums[8:16] + sums[16:24])[:rows]


def lane_of(rows, per_group):
    lane = lax.rem(lax.broadcasted_iota(jnp.int32, (rows, 128), 1), per_group)
    return lane == lax.broadcasted_iota(jnp.int32, (rows, 128), 0)


def pack_groups(tiles, per_group):
    mask = lane_of(tiles.shape[0], per_group)
    return jnp.sum(jnp.where(mask, tiles, 0.0), axis=0, keepdims=True)


def unpack_groups(center, spread, rows, per_group):
    mask = lane_of(rows, per_group)
    picked = [jnp.where(mask, jnp.broadcast_to(row, (rows, 128)), 0.0) for row in (center, spread)]
    sums = group_sum(jnp.concatenate(picked, axis=0), per_group)
    return sums[:rows], sums[rows:] * (1.0 / (LOCAL * DEVICES * per_group))


def merge_cores(src, other, per_group):
    tiles = GROUPS * per_group // 128
    off = other - src
    lane = lax.rem(lax.broadcasted_iota(jnp.int32, (1, 128), 1), per_group)
    squares = pltpu.roll(off * off * (0.5 * LOCAL * per_group), tiles, 1)
    return jnp.where(lane < tiles, src + 0.5 * off, src + other + squares)


def merge_direct(src, slots, entries, per_group):
    tiles = GROUPS * per_group // 128
    count = slots.shape[0] + 1
    own = src[...]
    off = slots[:, 0] - own
    total = jnp.sum(off, axis=0, keepdims=True)
    squares = jnp.sum(off * off, axis=0, keepdims=True) - total * total * (1.0 / count)
    lane = lax.rem(lax.broadcasted_iota(jnp.int32, (1, 128), 1), per_group)
    joined = jnp.where(lane < tiles, own + total * (1.0 / count), own * count + total)
    picked = [
        jnp.where(lane_of(rows, per_group), jnp.broadcast_to(row, (rows, 128)), 0.0)
        for rows, row in ((2 * tiles, joined), (tiles, squares))
    ]
    sums = group_sum(jnp.concatenate(picked, axis=0), per_group)
    spread = sums[tiles : 2 * tiles] + entries * sums[2 * tiles :]
    return sums[:tiles], spread * (1.0 / (LOCAL * DEVICES * per_group))


def local_stats(cells, src):
    channels = cells.shape[-1]
    per_group = channels // GROUPS
    center = jnp.sum(cells, axis=0, keepdims=True) * (1.0 / LOCAL)
    off = cells - center
    spread = as_tiles(jnp.sum(off * off, axis=0, keepdims=True))
    center = as_tiles(center)
    mean = group_sum(center, per_group) * (1.0 / per_group)
    off = center - mean
    spread = group_sum(spread + LOCAL * (off * off), per_group)
    if src.shape[0] == 1:
        src[...] = pack_groups(jnp.concatenate([mean, spread], axis=0), per_group)
    else:
        src[0:1] = pack_groups(mean, per_group)
        src[1:2] = pack_groups(spread, per_group)


class Activation:
    def __init__(self, raw, act, mean, variance, gain, shift):
        self.raw, self.act = raw, act
        self.center = as_row(mean)
        self.scale = as_row(lax.rsqrt(variance + EPSILON) * gain * 0.5)
        self.offset = as_row(shift * 0.5)

    def cell(self, r, c):
        half = (self.raw[r, c].astype(F32) - self.center) * self.scale + self.offset
        value = half + half * jnp.tanh(half)
        inside = None
        for at, extent, index, count in (
            (r, HALO_ROWS, lax.axis_index("ha"), NH),
            (c, HALO_COLS, lax.axis_index("wa"), NX * NZ),
        ):
            if at in (0, extent - 1):
                here = index > 0 if at == 0 else index < count - 1
                inside = here if inside is None else jnp.logical_and(inside, here)
        if inside is not None:
            value = jnp.where(inside, value, 0.0)
        self.act[r, c] = value.astype(BF16)


TAPS = ((1, 1), (0, 1), (2, 1), (1, 0), (1, 2), (0, 0), (0, 2), (2, 0), (2, 2))


def convolve(activation, weight, first, delayed):
    act = activation.act
    channels = act.shape[-1]
    made = set()
    result = first
    for time_off in range(3):
        total = None
        for row_off, col_off in TAPS:
            for r in range(row_off, row_off + ROWS):
                for c in range(col_off, col_off + COLS):
                    if (r, c) not in made:
                        activation.cell(r, c)
                        made.add((r, c))
            window = act[row_off : row_off + ROWS, col_off : col_off + COLS]
            product = jnp.dot(
                window.reshape(LOCAL, channels),
                weight[time_off, row_off, col_off],
                preferred_element_type=F32,
            )
            total = product if total is None else total + product
        total = total.reshape(CELLS, FRAMES, CO)
        late = 2 - time_off
        if late:
            delayed[late - 1, :, 8:, :] = total
            total = delayed[late - 1, :, 8 - late : 8 - late + FRAMES, :]
        result = result + total
    return result


def stage_cache(cache, wide, rows_ref, edge_ref, edge_wide):
    edge_wide[...] = jnp.zeros_like(edge_wide)
    wide[...] = jnp.zeros_like(wide)
    for frame in range(2):
        for c in range(COLS):
            both = cache[frame, c].astype(F32)
            for r in range(ROWS):
                wide[frame, 1 + r, 1 + c : 2 + c, :] = both[r : r + 1]
            if c in (0, COLS - 1):
                edge_wide[min(c, 1), frame * ROWS : frame * ROWS + ROWS, :] = both
        for r in range(ROWS):
            rows_ref[r, frame] = wide[frame, 1 + r, 1:17, :].astype(BF16)
    edge_ref[...] = edge_wide[...].astype(BF16)


def shift_cache(got_rows, got_edge, wide, shifted):
    row, across = lax.axis_index("ha"), lax.axis_index("wa")
    for frame in range(2):
        for r in range(HALO_ROWS):
            inside = {0: row > 0, HALO_ROWS - 1: row < NH - 1}.get(r)
            if inside is None:
                source, entry = 1, frame * ROWS + r - 1
            else:
                upper = r == 0
                own = got_rows[0 if upper else 1, frame].astype(F32)[0:COLS]
                wide[frame, r, 1 : COLS + 1, :] = jnp.where(inside, own, 0.0)
                source, entry = (2, frame * ROWS + ROWS - 1) if upper else (0, frame * ROWS)
            for slot, at, here in ((0, 0, across > 0), (1, COLS + 1, across < NX * NZ - 1)):
                edge = got_edge[source, slot].astype(F32)[entry : entry + 1]
                ok = here if inside is None else jnp.logical_and(here, inside)
                wide[frame, r, at : at + 1, :] = jnp.where(ok, edge, 0.0)
    for k in range(3):
        for frame in range(2):
            for r in range(HALO_ROWS):
                shifted[k, frame, r] = wide[frame, r, k : k + 16, :].astype(BF16)


def convolve_cache(shifted, weight, spill):
    channels = shifted.shape[-1]
    both, later = None, None
    for row_off in range(3):
        for k in range(3):
            two = shifted[k, :, row_off : row_off + ROWS].reshape(2 * ROWS * 16, channels)
            one = shifted[k, 1, row_off : row_off + ROWS].reshape(ROWS * 16, channels)
            a = jnp.dot(two, weight[0, row_off, k], preferred_element_type=F32)
            b = jnp.dot(one, weight[1, row_off, k], preferred_element_type=F32)
            both = a if both is None else both + a
            later = b if later is None else later + b
    half = ROWS * 16
    spill[...] = jnp.zeros_like(spill)
    for q in range(CO // 128):
        lanes = slice(128 * q, 128 * q + 128)
        spill[q, 0:half] = both[0:half, lanes] + later[:, lanes]
        spill[q, half : 2 * half] = both[half:, lanes]


def add_cache(spill, total):
    for r in range(ROWS):
        for c in range(COLS):
            for q in range(CO // 128):
                lanes = slice(128 * q, 128 * q + 128)
                total[r * COLS + c, 0:8, lanes] += spill[
                    q, pl.ds(r * 16 + c, 8, stride=ROWS * 16)
                ]


def kernel(
    features, cache_one, gain_one_in, shift_one_in, weight_one, cache_two, gain_two_in, shift_two_in, weight_two,
    bias_in, skip,
    out,
    gain_one, shift_one, gain_two, shift_two, bias,
    feats, wide_feats, cells_one, act_one, cells_two, act_two, w_one, w_two, w_skip,
    c_one, c_two, edge_wide_one, edge_wide_two, rows_one, rows_two, edge_one, edge_two,
    got_rows_one, got_rows_two, got_edge_one, got_edge_two,
    wide_one, wide_two, shifted_one, shifted_two, spill, base_one, base_two, delayed,
    src_1a, src_1b, src_core, got_core, src_two, slots_1a, slots_1b, slots_two,
    load, stat_send, stat_recv, halo_send, halo_recv,
):
    first_step = len(STAGES[0]) + 1
    loads = [
        pltpu.make_async_copy(features, feats, load.at[0]),
        pltpu.make_async_copy(cache_one, c_one, load.at[1]),
        pltpu.make_async_copy(cache_two, c_two, load.at[2]),
        pltpu.make_async_copy(skip, w_skip, load.at[3]),
    ]
    loads += [
        pltpu.make_async_copy(weight_one.at[i], w_one.at[i], load.at[4 + i]) for i in range(3)
    ]
    loads += [
        pltpu.make_async_copy(weight_two.at[i], w_two.at[i], load.at[7 + i]) for i in range(3)
    ]
    vectors = ((gain_one_in, gain_one), (shift_one_in, shift_one), (gain_two_in, gain_two),
               (shift_two_in, shift_two), (bias_in, bias))
    loads += [pltpu.make_async_copy(*pair, load.at[10 + n]) for n, pair in enumerate(vectors)]
    loads[0].start()

    barrier = pltpu.get_barrier_semaphore()
    greeted = [partner(offset) for offset in sorted(sum(STAGES, ()), key=lambda offset: -hops(offset))]
    greeted += [neighbour(side) for side in SIDES if side[1] != 0]
    for device in greeted:
        pl.semaphore_signal(barrier, inc=1, device_id=device, device_id_type=MESH)
    for copy in loads[1:]:
        copy.start()

    loads[0].wait()
    for t in range(FRAMES):
        for c in range(COLS):
            at = (t * COLS + c) * ROWS
            both = feats[t, c].astype(F32)
            for q in range(CI // 128):
                wide_feats[q, at : at + ROWS, :] = both[:, 128 * q : 128 * q + 128]
    for r in range(ROWS):
        for c in range(COLS):
            for q in range(CI // 128):
                lanes = slice(128 * q, 128 * q + 128)
                cells_one[1 + r, 1 + c, :, lanes] = wide_feats[
                    q, pl.ds(c * ROWS + r, FRAMES, stride=CELLS)
                ].astype(BF16)
    own = cells_one[1 : 1 + ROWS, 1 : 1 + COLS].reshape(LOCAL, CI)
    local_stats(own.astype(F32), src_1a)
    pl.semaphore_wait(barrier, len(greeted))

    send_stats(STAGES[0], src_1a, slots_1a, stat_send.at[0], stat_recv.at[0])
    halo_one = [halo_copy(cells_one, n, halo_send.at[0], halo_recv.at[0]) for n in range(8)]
    cached_one = [
        cache_copy(rows_one, edge_one, got_rows_one, got_edge_one, n, halo_send.at[1], halo_recv.at[1])
        for n in range(8)
    ]
    cached_two = [
        cache_copy(rows_two, edge_two, got_rows_two, got_edge_two, n, halo_send.at[2], halo_recv.at[2])
        for n in range(8)
    ]
    for copy in halo_one:
        copy.start()
    loads[1].wait()
    loads[2].wait()
    stage_cache(c_one, wide_one, rows_one, edge_one, edge_wide_one)
    for copy in cached_one:
        copy.start()
    stage_cache(c_two, wide_two, rows_two, edge_two, edge_wide_two)
    for copy in cached_two:
        copy.start()

    for copy in loads[10:] + loads[3:4]:
        copy.wait()
    own = cells_one[1 : 1 + ROWS, 1 : 1 + COLS].reshape(LOCAL, CI)
    shortcut = jnp.dot(own, w_skip[...], preferred_element_type=F32) + as_row(bias[...])
    base_two[...] = shortcut.reshape(CELLS, FRAMES, CO)

    wait_all(slots_1a, stat_recv.at[0])
    src_1b[0:1], src_1b[1:2] = merge_stats(src_1a, slots_1a, LOCAL * CI // GROUPS)
    send_stats(STAGES[1], src_1b, slots_1b, stat_send.at[1], stat_recv.at[1])

    for copy in cached_one:
        copy.wait_recv()
    for n in (4, 5):
        loads[n].wait()
    shift_cache(got_rows_one, got_edge_one, wide_one, shifted_one)
    convolve_cache(shifted_one, w_one, spill)
    base_one[...] = jnp.zeros_like(base_one)
    add_cache(spill, base_one)

    loads[6].wait()
    delayed[:, :, 0:8, :] = jnp.zeros_like(delayed[:, :, 0:8, :])
    for copy in halo_one:
        copy.wait_recv()
    wait_all(slots_1b, stat_recv.at[1])
    center, spread = merge_stats(src_1b, slots_1b, LOCAL * first_step * CI // GROUPS)
    mean, variance = unpack_groups(center, spread, CI // 128, CI // GROUPS)
    activation = Activation(cells_one, act_one, mean, variance, gain_one[...], shift_one[...])
    middle = convolve(activation, w_one, base_one[...], delayed).astype(BF16)
    cells_two[1 : 1 + ROWS, 1 : 1 + COLS] = middle.reshape(ROWS, COLS, FRAMES, CO)
    local_stats(middle.astype(F32).reshape(LOCAL, CO), src_core)
    row, across = lax.axis_index("ha"), lax.axis_index("wa")
    swap = pltpu.make_async_remote_copy(
        src_ref=src_core,
        dst_ref=got_core,
        send_sem=stat_send.at[3],
        recv_sem=stat_recv.at[3],
        device_id=(row + 1 - 2 * lax.rem(row, 2), across),
        device_id_type=MESH,
    )
    swap.start()
    swap.wait()
    src_two[...] = merge_cores(src_core[...], got_core[...], CO // GROUPS)
    halo_two = [halo_copy(cells_two, n, halo_send.at[3], halo_recv.at[3]) for n in range(8)]
    send_stats(DIRECT, src_two, slots_two, stat_send.at[2], stat_recv.at[2], end=FAR)
    for copy in halo_two:
        copy.start()
    send_stats(DIRECT, src_two, slots_two, stat_send.at[2], stat_recv.at[2], begin=FAR)

    for copy in cached_two:
        copy.wait_recv()
    for n in (7, 8):
        loads[n].wait()
    shift_cache(got_rows_two, got_edge_two, wide_two, shifted_two)
    convolve_cache(shifted_two, w_two, spill)
    add_cache(spill, base_two)

    loads[9].wait()
    for copy in halo_one + cached_one + cached_two + halo_two:
        copy.wait_send()
    wait_all(slots_1a, stat_send.at[0])
    wait_all(slots_1b, stat_send.at[1])
    for copy in halo_two:
        copy.wait_recv()
    wait_all(slots_two, stat_recv.at[2])
    mean, variance = merge_direct(src_two, slots_two, 2 * LOCAL * CO // GROUPS, CO // GROUPS)
    activation = Activation(cells_two, act_two, mean, variance, gain_two[...], shift_two[...])
    decoded = convolve(activation, w_two, base_two[...], delayed)
    out[...] = decoded.reshape(ROWS, COLS, FRAMES, CO).astype(BF16)
    wait_all(slots_two, stat_send.at[2])


def by_column(tile):
    return jnp.transpose(tile, (0, 2, 1, 3))


def on_device(
    features, first_cache, first_gain, first_shift, first_weight,
    second_cache, second_gain, second_shift, second_weight, second_bias, skip_weight,
):
    vmem = pl.BlockSpec(memory_space=pltpu.VMEM)
    hbm = pl.BlockSpec(memory_space=pltpu.HBM)
    cells = (HALO_ROWS, HALO_COLS, FRAMES)

    def per_conv(channels):
        return [
            pltpu.VMEM((2, COLS, ROWS, channels), BF16),
            pltpu.VMEM((2, 16, channels), F32),
            pltpu.VMEM((ROWS, 2, 16, channels), BF16),
            pltpu.VMEM((2, 16, channels), BF16),
            pltpu.VMEM((2, 2, 16, channels), BF16),
            pltpu.VMEM((3, 2, 16, channels), BF16),
            pltpu.VMEM((2, HALO_ROWS, 24, channels), F32),
            pltpu.VMEM((3, 2, HALO_ROWS, 16, channels), BF16),
        ]

    one, two = per_conv(CI), per_conv(CO)
    paired = [scratch for pair in zip(one, two) for scratch in pair]
    out = pl.pallas_call(
        kernel,
        out_shape=pltpu.VMEM((ROWS, COLS, FRAMES, CO), BF16),
        in_specs=[hbm] * 11,
        out_specs=vmem,
        scratch_shapes=[
            pltpu.VMEM((CI // 128, 128), F32),
            pltpu.VMEM((CI // 128, 128), F32),
            pltpu.VMEM((CO // 128, 128), F32),
            pltpu.VMEM((CO // 128, 128), F32),
            pltpu.VMEM((CO // 128, 128), F32),
            pltpu.VMEM((FRAMES, COLS, ROWS, CI), BF16),
            pltpu.VMEM((CI // 128, LOCAL, 128), F32),
            pltpu.VMEM(cells + (CI,), BF16),
            pltpu.VMEM(cells + (CI,), BF16),
            pltpu.VMEM(cells + (CO,), BF16),
            pltpu.VMEM(cells + (CO,), BF16),
            pltpu.VMEM((3, 3, 3, CI, CO), BF16),
            pltpu.VMEM((3, 3, 3, CO, CO), BF16),
            pltpu.VMEM((CI, CO), BF16),
            *paired,
            pltpu.VMEM((CO // 128, 8 * ROWS * 16, 128), F32),
            pltpu.VMEM((CELLS, FRAMES, CO), F32),
            pltpu.VMEM((CELLS, FRAMES, CO), F32),
            pltpu.VMEM((2, CELLS, FRAMES + 8, CO), F32),
            pltpu.VMEM((2, 128), F32),
            pltpu.VMEM((2, 128), F32),
            pltpu.VMEM((1, 128), F32),
            pltpu.VMEM((1, 128), F32),
            pltpu.VMEM((1, 128), F32),
            pltpu.VMEM((len(STAGES[0]), 2, 128), F32),
            pltpu.VMEM((len(STAGES[1]), 2, 128), F32),
            pltpu.VMEM((len(DIRECT), 1, 128), F32),
            pltpu.SemaphoreType.DMA((15,)),
            pltpu.SemaphoreType.DMA((4,)),
            pltpu.SemaphoreType.DMA((4,)),
            pltpu.SemaphoreType.DMA((4, 8)),
            pltpu.SemaphoreType.DMA((4, 8)),
        ],
        compiler_params=pltpu.CompilerParams(
            collective_id=0, has_side_effects=True, vmem_limit_bytes=63 << 20
        ),
        cost_estimate=pl.CostEstimate(
            flops=2 * LOCAL * CO * (27 * CI + 27 * CO + CI),
            bytes_accessed=2 * (27 * (CI + CO) + CI) * CO + 2 * LOCAL * (CI + CO),
            transcendentals=48 * FRAMES * (CI + CO),
        ),
    )(
        by_column(features),
        by_column(first_cache),
        first_gain.reshape(CI // 128, 128),
        first_shift.reshape(CI // 128, 128),
        first_weight,
        by_column(second_cache),
        second_gain.reshape(CO // 128, 128),
        second_shift.reshape(CO // 128, 128),
        second_weight,
        second_bias.reshape(CO // 128, 128),
        skip_weight,
    )
    return jnp.transpose(out, (2, 0, 1, 3))


def solution(mesh):
    tile = P(None, "ha", "wa", None)
    return jax.shard_map(
        on_device,
        mesh=mesh,
        in_specs=(tile, tile, P(), P(), P(), tile, P(), P(), P(), P(), P()),
        out_specs=tile,
        check_vma=False,
    )
```

```python
import functools

import jax
import jax.numpy as jnp
from jax import lax
from jax.experimental import pallas as pl
from jax.experimental.pallas import tpu as pltpu
from jax.sharding import PartitionSpec as P

F32 = jnp.float32
BF16 = jnp.bfloat16
MESH = pl.DeviceIdType.MESH
EPSILON = 1e-06

FRAMES = 16
ROWS, COLS = 2, 10
HALO_ROWS, HALO_COLS = ROWS + 2, COLS + 2
CELLS = ROWS * COLS
CI, CO = 512, 256
GROUPS = 32
NH, NX, NZ = 8, 4, 8
LOCAL = FRAMES * CELLS
DEVICES = NH * NX * NZ

def hops(offset):
    row, x, z = offset
    return min(row, NH - row) / 2 + min(x, NX - x) + min(z, NZ - z)


STAGES = tuple(
    tuple(sorted(stage, key=lambda offset: -hops(offset)))
    for stage in (
        [(0, 0, c) for c in range(1, NZ)],
        [(a, b, 0) for a in range(NH) for b in range(NX) if (a, b) != (0, 0)],
    )
)
CHIPS = sorted(
    (
        (a, b, c)
        for a in range(0, NH, 2)
        for b in range(NX)
        for c in range(NZ)
        if (a, b, c) != (0, 0, 0)
    ),
    key=lambda offset: -hops(offset),
)
FAR = [offset for offset in CHIPS if hops(offset) >= 6]
NEAR = CHIPS[len(FAR) :]
HALO_AT = sum(hops(offset) >= 4 for offset in NEAR)
SIDES = tuple((a, b) for a in (-1, 0, 1) for b in (-1, 0, 1) if (a, b) != (0, 0))


def place():
    across = lax.axis_index("wa")
    return lax.axis_index("ha"), lax.rem(across, NX), lax.div(across, NX)


def partner(offset):
    row, x, z = place()
    return (
        lax.rem(row + offset[0], NH),
        lax.rem(z + offset[2], NZ) * NX + lax.rem(x + offset[1], NX),
    )


def other_core(row):
    return row + 1 - 2 * lax.rem(row, 2)


def neighbour(side):
    row, across = lax.axis_index("ha"), lax.axis_index("wa")
    return lax.rem(row + side[0] + NH, NH), lax.rem(across + side[1] + NX * NZ, NX * NZ)


def span(step, extent):
    if step == 0:
        return pl.ds(1, extent), pl.ds(1, extent)
    if step < 0:
        return pl.ds(1, 1), pl.ds(extent + 1, 1)
    return pl.ds(extent, 1), pl.ds(0, 1)


def halo_copy(ref, number, send, recv):
    side = SIDES[number]
    row_from, row_to = span(side[0], ROWS)
    col_from, col_to = span(side[1], COLS)
    return pltpu.make_async_remote_copy(
        src_ref=ref.at[row_from, col_from],
        dst_ref=ref.at[row_to, col_to],
        send_sem=send.at[number],
        recv_sem=recv.at[number],
        device_id=neighbour(side),
        device_id_type=MESH,
    )


def cache_copy(rows_ref, edge_ref, got_rows, got_edge, number, send, recv):
    down, right = SIDES[number]
    if right == 0:
        src = rows_ref.at[0 if down < 0 else 1]
        dst = got_rows.at[1 if down < 0 else 0]
    else:
        src = edge_ref.at[0 if right < 0 else 1]
        dst = got_edge.at[down + 1, 1 if right < 0 else 0]
    return pltpu.make_async_remote_copy(
        src_ref=src,
        dst_ref=dst,
        send_sem=send.at[number],
        recv_sem=recv.at[number],
        device_id=neighbour(SIDES[number]),
        device_id_type=MESH,
    )


def send_row(src, dst, send, recv, device):
    pltpu.make_async_remote_copy(
        src_ref=src, dst_ref=dst, send_sem=send, recv_sem=recv, device_id=device, device_id_type=MESH
    ).start()


def send_stats(offsets, src, slots, send, recv, begin=0, end=None):
    for number, offset in list(enumerate(offsets))[begin:end]:
        send_row(src, slots.at[number], send, recv, partner(offset))


def send_far(src, slots, send, recv):
    for number, offset in enumerate(FAR):
        row, across = partner(offset)
        send_row(src, slots.at[2 * number], send, recv, (row, across))
        send_row(src, slots.at[2 * number + 1], send, recv, (other_core(row), across))


def wait_all(slots, sem):
    pltpu.make_async_copy(slots, slots, sem).wait()


def merge_stats(src, slots, entries):
    count = slots.shape[0] + 1
    own = src[...]
    others = slots[...]
    total = own + jnp.sum(others, axis=0)
    center = total[0:1] / count
    off = own[0:1] - center
    offs = others[:, 0] - center
    squares = off * off + jnp.sum(offs * offs, axis=0, keepdims=True)
    return center, total[1:2] + entries * squares


def as_tiles(row):
    return jnp.concatenate(
        [row[:, 128 * q : 128 * q + 128] for q in range(row.shape[1] // 128)], axis=0
    )


def as_row(tiles):
    return jnp.concatenate([tiles[q : q + 1] for q in range(tiles.shape[0])], axis=1)


def group_sum(tiles, per_group):
    rows = tiles.shape[0]
    first = lax.div(lax.broadcasted_iota(jnp.int32, (128, 128), 0), per_group)
    second = lax.div(lax.broadcasted_iota(jnp.int32, (128, 128), 1), per_group)
    same = jnp.where(first == second, 1.0, 0.0).astype(BF16)
    if rows < 8:
        tiles = jnp.concatenate([tiles, jnp.zeros((8 - rows, 128), F32)], axis=0)
    high = tiles.astype(BF16).astype(F32)
    rest = tiles - high
    middle = rest.astype(BF16).astype(F32)
    terms = jnp.concatenate([high, middle, rest - middle], axis=0).astype(BF16)
    sums = jnp.dot(terms, same, preferred_element_type=F32)
    return (sums[0:8] + sums[8:16] + sums[16:24])[:rows]


def lane_of(rows, per_group):
    lane = lax.rem(lax.broadcasted_iota(jnp.int32, (rows, 128), 1), per_group)
    return lane == lax.broadcasted_iota(jnp.int32, (rows, 128), 0)


def pack_groups(tiles, per_group):
    mask = lane_of(tiles.shape[0], per_group)
    return jnp.sum(jnp.where(mask, tiles, 0.0), axis=0, keepdims=True)


def spread_lane(rows, lane, per_group):
    at = lax.broadcasted_iota(jnp.int32, rows.shape, 1)
    return jnp.take_along_axis(rows, at - lax.rem(at, per_group) + lane, axis=1)


def unpack_groups(row, count, first, per_group):
    number = lax.broadcasted_iota(jnp.int32, (8, 128), 0)
    number = jnp.where(number < count, number, 0) + first
    return spread_lane(jnp.broadcast_to(row, (8, 128)), number, per_group)[:count]


def merge_cores(src, other, per_group):
    tiles = GROUPS * per_group // 128
    off = other - src
    lane = lax.rem(lax.broadcasted_iota(jnp.int32, (1, 128), 1), per_group)
    squares = pltpu.roll(off * off * (0.5 * LOCAL * per_group), tiles, 1)
    return jnp.where(lane < tiles, src + 0.5 * off, src + other + squares)


def merge_direct(src, near, far, per_group):
    tiles = GROUPS * per_group // 128
    own = src[...]
    near_off, far_off = near[:, 0] - own, far[:, 0] - own
    near_sum = jnp.sum(near_off, axis=0, keepdims=True)
    far_sum = jnp.sum(far_off, axis=0, keepdims=True)
    total = 2.0 * near_sum + far_sum
    squares = 2.0 * jnp.sum(near_off * near_off, axis=0, keepdims=True)
    squares += jnp.sum(far_off * far_off, axis=0, keepdims=True)
    squares -= total * total * (1.0 / DEVICES)
    rows = 1 + near.shape[0] + far.shape[0]
    mean = unpack_groups(own + total * (1.0 / DEVICES), tiles, 0, per_group)
    spread = unpack_groups(near_sum + far_sum + rows * own, tiles, tiles, per_group)
    spread += (LOCAL * per_group) * unpack_groups(squares, tiles, 0, per_group)
    return mean, spread * (1.0 / (LOCAL * DEVICES * per_group))


def local_stats(cells, src):
    channels = cells.shape[-1]
    per_group = channels // GROUPS
    center = jnp.sum(cells, axis=0, keepdims=True) * (1.0 / LOCAL)
    off = cells - center
    spread = as_tiles(jnp.sum(off * off, axis=0, keepdims=True))
    center = as_tiles(center)
    tiles = center.shape[0]
    mean = group_sum(center, per_group) * (1.0 / per_group)
    off = center - mean
    spread = group_sum(spread + LOCAL * (off * off), per_group)
    if src.shape[0] == 1:
        src[...] = pack_groups(jnp.concatenate([mean, spread], axis=0), per_group)
    else:
        src[0:1] = pack_groups(mean, per_group)
        src[1:2] = pack_groups(spread, per_group)


class Activation:
    def __init__(self, raw, act, mean, variance, gain, shift):
        self.raw, self.act = raw, act
        self.center = as_row(mean)
        self.scale = as_row(lax.rsqrt(variance + EPSILON) * gain * 0.5)
        self.offset = as_row(shift * 0.5)

    def cell(self, r, c):
        half = (self.raw[r, c].astype(F32) - self.center) * self.scale + self.offset
        value = half + half * jnp.tanh(half)
        inside = None
        for at, extent, index, count in (
            (r, HALO_ROWS, lax.axis_index("ha"), NH),
            (c, HALO_COLS, lax.axis_index("wa"), NX * NZ),
        ):
            if at in (0, extent - 1):
                here = index > 0 if at == 0 else index < count - 1
                inside = here if inside is None else jnp.logical_and(inside, here)
        if inside is not None:
            value = jnp.where(inside, value, 0.0)
        self.act[r, c] = value.astype(BF16)


TAPS = ((1, 1), (0, 1), (2, 1), (1, 0), (1, 2), (0, 0), (0, 2), (2, 0), (2, 2))


def convolve(activation, weight, first, delayed):
    act = activation.act
    channels = act.shape[-1]
    made = set()
    result = first
    for time_off in range(3):
        total = None
        for row_off, col_off in TAPS:
            for r in range(row_off, row_off + ROWS):
                for c in range(col_off, col_off + COLS):
                    if (r, c) not in made:
                        activation.cell(r, c)
                        made.add((r, c))
            window = act[row_off : row_off + ROWS, col_off : col_off + COLS]
            product = jnp.dot(
                window.reshape(LOCAL, channels),
                weight[time_off, row_off, col_off],
                preferred_element_type=F32,
            )
            total = product if total is None else total + product
        total = total.reshape(CELLS, FRAMES, CO)
        late = 2 - time_off
        if late:
            delayed[late - 1, :, 8:, :] = total
            total = delayed[late - 1, :, 8 - late : 8 - late + FRAMES, :]
        result = result + total
    return result


def stage_cache(cache, wide, rows_ref, edge_ref):
    wide[...] = jnp.zeros_like(wide)
    for frame in range(2):
        for c in range(COLS):
            both = cache[frame, c].astype(F32)
            for r in range(ROWS):
                wide[frame, 1 + r, 1 + c : 2 + c, :] = both[r : r + 1]
            if c in (0, COLS - 1):
                edge_ref[min(c, 1), frame * ROWS : frame * ROWS + ROWS, :] = both
        for r in range(ROWS):
            rows_ref[r, frame] = wide[frame, 1 + r, 1:17, :].astype(BF16)


def shift_cache(got_rows, got_edge, wide, shifted):
    row, across = lax.axis_index("ha"), lax.axis_index("wa")
    for frame in range(2):
        for r in range(HALO_ROWS):
            inside = {0: row > 0, HALO_ROWS - 1: row < NH - 1}.get(r)
            if inside is None:
                source, entry = 1, frame * ROWS + r - 1
            else:
                upper = r == 0
                own = got_rows[0 if upper else 1, frame].astype(F32)[0:COLS]
                wide[frame, r, 1 : COLS + 1, :] = jnp.where(inside, own, 0.0)
                source, entry = (2, frame * ROWS + ROWS - 1) if upper else (0, frame * ROWS)
            for slot, at, here in ((0, 0, across > 0), (1, COLS + 1, across < NX * NZ - 1)):
                edge = got_edge[source, slot, entry : entry + 1]
                ok = here if inside is None else jnp.logical_and(here, inside)
                wide[frame, r, at : at + 1, :] = jnp.where(ok, edge, 0.0)
    for k in range(3):
        for frame in range(2):
            for r in range(HALO_ROWS):
                shifted[k, frame, r] = wide[frame, r, k : k + 16, :].astype(BF16)


def convolve_cache(shifted, weight, spill):
    channels = shifted.shape[-1]
    both, later = None, None
    for row_off in range(3):
        for k in range(3):
            two = shifted[k, :, row_off : row_off + ROWS].reshape(2 * ROWS * 16, channels)
            one = shifted[k, 1, row_off : row_off + ROWS].reshape(ROWS * 16, channels)
            a = jnp.dot(two, weight[0, row_off, k], preferred_element_type=F32)
            b = jnp.dot(one, weight[1, row_off, k], preferred_element_type=F32)
            both = a if both is None else both + a
            later = b if later is None else later + b
    half = ROWS * 16
    spill[...] = jnp.zeros_like(spill)
    for q in range(CO // 128):
        lanes = slice(128 * q, 128 * q + 128)
        spill[q, 0:half] = both[0:half, lanes] + later[:, lanes]
        spill[q, half : 2 * half] = both[half:, lanes]


def add_cache(spill, total):
    for r in range(ROWS):
        for c in range(COLS):
            for q in range(CO // 128):
                lanes = slice(128 * q, 128 * q + 128)
                total[r * COLS + c, 0:8, lanes] += spill[
                    q, pl.ds(r * 16 + c, 8, stride=ROWS * 16)
                ]


def kernel(
    features, cache_one, gain_one_in, shift_one_in, weight_one, cache_two, gain_two_in, shift_two_in, weight_two,
    bias_in, skip,
    out,
    gain_one, shift_one, gain_two, shift_two, bias,
    feats, wide_feats, cells_one, act_one, cells_two, act_two, w_one, w_two, w_skip,
    c_one, c_two, rows_one, rows_two, edge_one, edge_two,
    got_rows_one, got_rows_two, got_edge_one, got_edge_two,
    wide_one, wide_two, shifted_one, shifted_two, spill, base_one, base_two, delayed,
    src_1a, src_1b, src_core, got_core, src_two, slots_1a, slots_1b, slots_two, slots_far,
    load, stat_send, stat_recv, halo_send, halo_recv,
):
    first_step = len(STAGES[0]) + 1
    loads = [
        pltpu.make_async_copy(features, feats, load.at[0]),
        pltpu.make_async_copy(cache_one, c_one, load.at[1]),
        pltpu.make_async_copy(cache_two, c_two, load.at[2]),
        pltpu.make_async_copy(skip, w_skip, load.at[3]),
    ]
    loads += [
        pltpu.make_async_copy(weight_one.at[i], w_one.at[i], load.at[4 + i]) for i in range(3)
    ]
    loads += [
        pltpu.make_async_copy(weight_two.at[i], w_two.at[i], load.at[7 + i]) for i in range(3)
    ]
    vectors = ((gain_one_in, gain_one), (shift_one_in, shift_one), (gain_two_in, gain_two),
               (shift_two_in, shift_two), (bias_in, bias))
    loads += [pltpu.make_async_copy(*pair, load.at[10 + n]) for n, pair in enumerate(vectors)]
    loads[0].start()

    barrier = pltpu.get_barrier_semaphore()
    greeted = [partner(offset) for offset in sorted(sum(STAGES, ()), key=lambda offset: -hops(offset))]
    greeted += [neighbour(side) for side in SIDES if side[1] != 0]
    for device in greeted:
        pl.semaphore_signal(barrier, inc=1, device_id=device, device_id_type=MESH)
    for copy in loads[1:]:
        copy.start()

    loads[0].wait()
    for t in range(FRAMES):
        for c in range(COLS):
            at = (t * COLS + c) * ROWS
            both = feats[t, c].astype(F32)
            for q in range(CI // 128):
                wide_feats[q, at : at + ROWS, :] = both[:, 128 * q : 128 * q + 128]
    for r in range(ROWS):
        for c in range(COLS):
            for q in range(CI // 128):
                lanes = slice(128 * q, 128 * q + 128)
                cells_one[1 + r, 1 + c, :, lanes] = wide_feats[
                    q, pl.ds(c * ROWS + r, FRAMES, stride=CELLS)
                ].astype(BF16)
    own = cells_one[1 : 1 + ROWS, 1 : 1 + COLS].reshape(LOCAL, CI)
    local_stats(own.astype(F32), src_1a)
    pl.semaphore_wait(barrier, len(greeted))

    send_stats(STAGES[0], src_1a, slots_1a, stat_send.at[0], stat_recv.at[0])
    halo_one = [halo_copy(cells_one, n, halo_send.at[0], halo_recv.at[0]) for n in range(8)]
    cached_one = [
        cache_copy(rows_one, edge_one, got_rows_one, got_edge_one, n, halo_send.at[1], halo_recv.at[1])
        for n in range(8)
    ]
    cached_two = [
        cache_copy(rows_two, edge_two, got_rows_two, got_edge_two, n, halo_send.at[2], halo_recv.at[2])
        for n in range(8)
    ]
    for copy in halo_one:
        copy.start()
    loads[1].wait()
    loads[2].wait()
    stage_cache(c_one, wide_one, rows_one, edge_one)
    for copy in cached_one:
        copy.start()
    stage_cache(c_two, wide_two, rows_two, edge_two)
    for copy in cached_two:
        copy.start()

    for copy in loads[10:] + loads[3:4]:
        copy.wait()
    own = cells_one[1 : 1 + ROWS, 1 : 1 + COLS].reshape(LOCAL, CI)
    shortcut = jnp.dot(own, w_skip[...], preferred_element_type=F32) + as_row(bias[...])
    base_two[...] = shortcut.reshape(CELLS, FRAMES, CO)

    wait_all(slots_1a, stat_recv.at[0])
    src_1b[0:1], src_1b[1:2] = merge_stats(src_1a, slots_1a, LOCAL * CI // GROUPS)
    send_stats(STAGES[1], src_1b, slots_1b, stat_send.at[1], stat_recv.at[1])

    for copy in cached_one:
        copy.wait_recv()
    for n in (4, 5):
        loads[n].wait()
    shift_cache(got_rows_one, got_edge_one, wide_one, shifted_one)
    convolve_cache(shifted_one, w_one, spill)
    base_one[...] = jnp.zeros_like(base_one)
    add_cache(spill, base_one)

    loads[6].wait()
    delayed[:, :, 0:8, :] = jnp.zeros_like(delayed[:, :, 0:8, :])
    for copy in halo_one:
        copy.wait_recv()
    wait_all(slots_1b, stat_recv.at[1])
    center, spread = merge_stats(src_1b, slots_1b, LOCAL * first_step * CI // GROUPS)
    mean = unpack_groups(center, CI // 128, 0, CI // GROUPS)
    variance = unpack_groups(spread * (GROUPS / (LOCAL * DEVICES * CI)), CI // 128, 0, CI // GROUPS)
    activation = Activation(cells_one, act_one, mean, variance, gain_one[...], shift_one[...])
    middle = convolve(activation, w_one, base_one[...], delayed).astype(BF16)
    cells_two[1 : 1 + ROWS, 1 : 1 + COLS] = middle.reshape(ROWS, COLS, FRAMES, CO)
    local_stats(middle.astype(F32).reshape(LOCAL, CO), src_core)
    row, across = lax.axis_index("ha"), lax.axis_index("wa")
    swap = pltpu.make_async_remote_copy(
        src_ref=src_core,
        dst_ref=got_core,
        send_sem=stat_send.at[3],
        recv_sem=stat_recv.at[3],
        device_id=(other_core(row), across),
        device_id_type=MESH,
    )
    swap.start()
    send_far(src_core, slots_far, stat_send.at[4], stat_recv.at[4])
    swap.wait()
    src_two[...] = merge_cores(src_core[...], got_core[...], CO // GROUPS)
    halo_two = [halo_copy(cells_two, n, halo_send.at[3], halo_recv.at[3]) for n in range(8)]
    send_stats(NEAR, src_two, slots_two, stat_send.at[2], stat_recv.at[2], end=HALO_AT)
    for copy in halo_two:
        copy.start()
    send_stats(NEAR, src_two, slots_two, stat_send.at[2], stat_recv.at[2], begin=HALO_AT)

    for copy in cached_two:
        copy.wait_recv()
    for n in (7, 8):
        loads[n].wait()
    shift_cache(got_rows_two, got_edge_two, wide_two, shifted_two)
    convolve_cache(shifted_two, w_two, spill)
    add_cache(spill, base_two)

    loads[9].wait()
    for copy in halo_one + cached_one + cached_two + halo_two:
        copy.wait_send()
    wait_all(slots_1a, stat_send.at[0])
    wait_all(slots_1b, stat_send.at[1])
    for copy in halo_two:
        copy.wait_recv()
    wait_all(slots_two, stat_recv.at[2])
    wait_all(slots_far, stat_recv.at[4])
    mean, variance = merge_direct(src_two, slots_two, slots_far, CO // GROUPS)
    activation = Activation(cells_two, act_two, mean, variance, gain_two[...], shift_two[...])
    decoded = convolve(activation, w_two, base_two[...], delayed)
    out[...] = decoded.reshape(ROWS, COLS, FRAMES, CO).astype(BF16)
    wait_all(slots_two, stat_send.at[2])
    wait_all(slots_far, stat_send.at[4])


def by_column(tile):
    return jnp.transpose(tile, (0, 2, 1, 3))


def on_device(
    features, first_cache, first_gain, first_shift, first_weight,
    second_cache, second_gain, second_shift, second_weight, second_bias, skip_weight,
):
    vmem = pl.BlockSpec(memory_space=pltpu.VMEM)
    hbm = pl.BlockSpec(memory_space=pltpu.HBM)
    cells = (HALO_ROWS, HALO_COLS, FRAMES)

    def per_conv(channels):
        return [
            pltpu.VMEM((2, COLS, ROWS, channels), BF16),
            pltpu.VMEM((ROWS, 2, 16, channels), BF16),
            pltpu.VMEM((2, 2 * ROWS, channels), F32),
            pltpu.VMEM((2, 2, 16, channels), BF16),
            pltpu.VMEM((3, 2, 2 * ROWS, channels), F32),
            pltpu.VMEM((2, HALO_ROWS, 24, channels), F32),
            pltpu.VMEM((3, 2, HALO_ROWS, 16, channels), BF16),
        ]

    one, two = per_conv(CI), per_conv(CO)
    paired = [scratch for pair in zip(one, two) for scratch in pair]
    out = pl.pallas_call(
        kernel,
        out_shape=pltpu.VMEM((ROWS, COLS, FRAMES, CO), BF16),
        in_specs=[hbm] * 11,
        out_specs=vmem,
        scratch_shapes=[
            pltpu.VMEM((CI // 128, 128), F32),
            pltpu.VMEM((CI // 128, 128), F32),
            pltpu.VMEM((CO // 128, 128), F32),
            pltpu.VMEM((CO // 128, 128), F32),
            pltpu.VMEM((CO // 128, 128), F32),
            pltpu.VMEM((FRAMES, COLS, ROWS, CI), BF16),
            pltpu.VMEM((CI // 128, LOCAL, 128), F32),
            pltpu.VMEM(cells + (CI,), BF16),
            pltpu.VMEM(cells + (CI,), BF16),
            pltpu.VMEM(cells + (CO,), BF16),
            pltpu.VMEM(cells + (CO,), BF16),
            pltpu.VMEM((3, 3, 3, CI, CO), BF16),
            pltpu.VMEM((3, 3, 3, CO, CO), BF16),
            pltpu.VMEM((CI, CO), BF16),
            *paired,
            pltpu.VMEM((CO // 128, 8 * ROWS * 16, 128), F32),
            pltpu.VMEM((CELLS, FRAMES, CO), F32),
            pltpu.VMEM((CELLS, FRAMES, CO), F32),
            pltpu.VMEM((2, CELLS, FRAMES + 8, CO), F32),
            pltpu.VMEM((2, 128), F32),
            pltpu.VMEM((2, 128), F32),
            pltpu.VMEM((1, 128), F32),
            pltpu.VMEM((1, 128), F32),
            pltpu.VMEM((1, 128), F32),
            pltpu.VMEM((len(STAGES[0]), 2, 128), F32),
            pltpu.VMEM((len(STAGES[1]), 2, 128), F32),
            pltpu.VMEM((len(NEAR), 1, 128), F32),
            pltpu.VMEM((2 * len(FAR), 1, 128), F32),
            pltpu.SemaphoreType.DMA((15,)),
            pltpu.SemaphoreType.DMA((5,)),
            pltpu.SemaphoreType.DMA((5,)),
            pltpu.SemaphoreType.DMA((4, 8)),
            pltpu.SemaphoreType.DMA((4, 8)),
        ],
        compiler_params=pltpu.CompilerParams(
            collective_id=0, has_side_effects=True, vmem_limit_bytes=63 << 20
        ),
        cost_estimate=pl.CostEstimate(
            flops=2 * LOCAL * CO * (27 * CI + 27 * CO + CI),
            bytes_accessed=2 * (27 * (CI + CO) + CI) * CO + 2 * LOCAL * (CI + CO),
            transcendentals=48 * FRAMES * (CI + CO),
        ),
    )(
        by_column(features),
        by_column(first_cache),
        first_gain.reshape(CI // 128, 128),
        first_shift.reshape(CI // 128, 128),
        first_weight,
        by_column(second_cache),
        second_gain.reshape(CO // 128, 128),
        second_shift.reshape(CO // 128, 128),
        second_weight,
        second_bias.reshape(CO // 128, 128),
        skip_weight,
    )
    return jnp.transpose(out, (2, 0, 1, 3))


def solution(mesh):
    tile = P(None, "ha", "wa", None)
    return jax.shard_map(
        on_device,
        mesh=mesh,
        in_specs=(tile, tile, P(), P(), P(), tile, P(), P(), P(), P(), P()),
        out_specs=tile,
        check_vma=False,
    )
```

```python
import functools

import jax
import jax.numpy as jnp
from jax import lax
from jax.experimental import pallas as pl
from jax.experimental.pallas import tpu as pltpu
from jax.sharding import PartitionSpec as P

F32 = jnp.float32
BF16 = jnp.bfloat16
MESH = pl.DeviceIdType.MESH
EPSILON = 1e-06

FRAMES = 16
ROWS, COLS = 2, 10
HALO_ROWS, HALO_COLS = ROWS + 2, COLS + 2
CELLS = ROWS * COLS
CI, CO = 512, 256
GROUPS = 32
NH, NX, NZ = 8, 4, 8
LOCAL = FRAMES * CELLS
DEVICES = NH * NX * NZ

def hops(offset):
    row, x, z = offset
    return min(row, NH - row) / 2 + min(x, NX - x) + min(z, NZ - z)


STAGES = tuple(
    tuple(sorted(stage, key=lambda offset: -hops(offset)))
    for stage in (
        [(0, 0, c) for c in range(1, NZ)],
        [(a, b, 0) for a in range(NH) for b in range(NX) if (a, b) != (0, 0)],
    )
)
CHIPS = sorted(
    (
        (a, b, c)
        for a in range(0, NH, 2)
        for b in range(NX)
        for c in range(NZ)
        if (a, b, c) != (0, 0, 0)
    ),
    key=lambda offset: -hops(offset),
)
FAR = [offset for offset in CHIPS if hops(offset) >= 6]
NEAR = CHIPS[len(FAR) :]
SIDES = tuple((a, b) for a in (-1, 0, 1) for b in (-1, 0, 1) if (a, b) != (0, 0))


def place():
    across = lax.axis_index("wa")
    return lax.axis_index("ha"), lax.rem(across, NX), lax.div(across, NX)


def partner(offset):
    row, x, z = place()
    return (
        lax.rem(row + offset[0], NH),
        lax.rem(z + offset[2], NZ) * NX + lax.rem(x + offset[1], NX),
    )


def other_core(row):
    return row + 1 - 2 * lax.rem(row, 2)


def neighbour(side):
    row, across = lax.axis_index("ha"), lax.axis_index("wa")
    return lax.rem(row + side[0] + NH, NH), lax.rem(across + side[1] + NX * NZ, NX * NZ)


def span(step, extent):
    if step == 0:
        return pl.ds(1, extent), pl.ds(1, extent)
    if step < 0:
        return pl.ds(1, 1), pl.ds(extent + 1, 1)
    return pl.ds(extent, 1), pl.ds(0, 1)


def halo_copy(ref, number, send, recv):
    side = SIDES[number]
    row_from, row_to = span(side[0], ROWS)
    col_from, col_to = span(side[1], COLS)
    return pltpu.make_async_remote_copy(
        src_ref=ref.at[row_from, col_from],
        dst_ref=ref.at[row_to, col_to],
        send_sem=send.at[number],
        recv_sem=recv.at[number],
        device_id=neighbour(side),
        device_id_type=MESH,
    )


def cache_copy(rows_ref, edge_ref, got_rows, got_edge, number, send, recv):
    down, right = SIDES[number]
    if right == 0:
        src = rows_ref.at[0 if down < 0 else 1]
        dst = got_rows.at[1 if down < 0 else 0]
    else:
        src = edge_ref.at[0 if right < 0 else 1]
        dst = got_edge.at[down + 1, 1 if right < 0 else 0]
    return pltpu.make_async_remote_copy(
        src_ref=src,
        dst_ref=dst,
        send_sem=send.at[number],
        recv_sem=recv.at[number],
        device_id=neighbour(SIDES[number]),
        device_id_type=MESH,
    )


def send_row(src, dst, send, recv, device):
    pltpu.make_async_remote_copy(
        src_ref=src, dst_ref=dst, send_sem=send, recv_sem=recv, device_id=device, device_id_type=MESH
    ).start()


def send_stats(offsets, src, slots, send, recv, begin=0, end=None):
    for number, offset in list(enumerate(offsets))[begin:end]:
        send_row(src, slots.at[number], send, recv, partner(offset))


def send_far(src, slots, send, recv):
    for number, offset in enumerate(FAR):
        row, across = partner(offset)
        send_row(src, slots.at[2 * number], send, recv, (row, across))
        send_row(src, slots.at[2 * number + 1], send, recv, (other_core(row), across))


def wait_all(slots, sem):
    pltpu.make_async_copy(slots, slots, sem).wait()


def merge_stats(src, slots, entries):
    count = slots.shape[0] + 1
    own = src[...]
    others = slots[...]
    total = own + jnp.sum(others, axis=0)
    center = total[0:1] / count
    off = own[0:1] - center
    offs = others[:, 0] - center
    squares = off * off + jnp.sum(offs * offs, axis=0, keepdims=True)
    return center, total[1:2] + entries * squares


def as_tiles(row):
    return jnp.concatenate(
        [row[:, 128 * q : 128 * q + 128] for q in range(row.shape[1] // 128)], axis=0
    )


def as_row(tiles):
    return jnp.concatenate([tiles[q : q + 1] for q in range(tiles.shape[0])], axis=1)


def group_sum(tiles, per_group):
    rows = tiles.shape[0]
    first = lax.div(lax.broadcasted_iota(jnp.int32, (128, 128), 0), per_group)
    second = lax.div(lax.broadcasted_iota(jnp.int32, (128, 128), 1), per_group)
    same = jnp.where(first == second, 1.0, 0.0).astype(BF16)
    if rows < 8:
        tiles = jnp.concatenate([tiles, jnp.zeros((8 - rows, 128), F32)], axis=0)
    high = tiles.astype(BF16).astype(F32)
    rest = tiles - high
    middle = rest.astype(BF16).astype(F32)
    terms = jnp.concatenate([high, middle, rest - middle], axis=0).astype(BF16)
    sums = jnp.dot(terms, same, preferred_element_type=F32)
    return (sums[0:8] + sums[8:16] + sums[16:24])[:rows]


def lane_of(rows, per_group):
    lane = lax.rem(lax.broadcasted_iota(jnp.int32, (rows, 128), 1), per_group)
    return lane == lax.broadcasted_iota(jnp.int32, (rows, 128), 0)


def pack_groups(tiles, per_group):
    mask = lane_of(tiles.shape[0], per_group)
    return jnp.sum(jnp.where(mask, tiles, 0.0), axis=0, keepdims=True)


def spread_lane(rows, lane, per_group):
    at = lax.broadcasted_iota(jnp.int32, rows.shape, 1)
    return jnp.take_along_axis(rows, at - lax.rem(at, per_group) + lane, axis=1)


def unpack_groups(row, count, first, per_group):
    number = lax.broadcasted_iota(jnp.int32, (8, 128), 0)
    number = jnp.where(number < count, number, 0) + first
    return spread_lane(jnp.broadcast_to(row, (8, 128)), number, per_group)[:count]


def merge_cores(src, other, per_group):
    tiles = GROUPS * per_group // 128
    off = other - src
    lane = lax.rem(lax.broadcasted_iota(jnp.int32, (1, 128), 1), per_group)
    squares = pltpu.roll(off * off * (0.5 * LOCAL * per_group), tiles, 1)
    return jnp.where(lane < tiles, src + 0.5 * off, src + other + squares)


def deviations(own, slots):
    off = slots[:, 0] - own
    return jnp.sum(off, axis=0, keepdims=True), jnp.sum(off * off, axis=0, keepdims=True)


def merge_direct(own, near, far, rows, per_group):
    tiles = GROUPS * per_group // 128
    total = 2.0 * near[0] + far[0]
    squares = 2.0 * near[1] + far[1] - total * total * (1.0 / DEVICES)
    mean = unpack_groups(own + total * (1.0 / DEVICES), tiles, 0, per_group)
    spread = unpack_groups(near[0] + far[0] + rows * own, tiles, tiles, per_group)
    spread += (LOCAL * per_group) * unpack_groups(squares, tiles, 0, per_group)
    return mean, spread * (1.0 / (LOCAL * DEVICES * per_group))


def local_stats(cells, src):
    channels = cells.shape[-1]
    per_group = channels // GROUPS
    center = jnp.sum(cells, axis=0, keepdims=True) * (1.0 / LOCAL)
    off = cells - center
    spread = as_tiles(jnp.sum(off * off, axis=0, keepdims=True))
    center = as_tiles(center)
    tiles = center.shape[0]
    mean = group_sum(center, per_group) * (1.0 / per_group)
    off = center - mean
    spread = group_sum(spread + LOCAL * (off * off), per_group)
    if src.shape[0] == 1:
        src[...] = pack_groups(jnp.concatenate([mean, spread], axis=0), per_group)
    else:
        src[0:1] = pack_groups(mean, per_group)
        src[1:2] = pack_groups(spread, per_group)


class Activation:
    def __init__(self, raw, act, mean, variance, gain, shift):
        self.raw, self.act = raw, act
        self.center = as_row(mean)
        self.scale = as_row(lax.rsqrt(variance + EPSILON) * gain * 0.5)
        self.offset = as_row(shift * 0.5)

    def cell(self, r, c):
        half = (self.raw[r, c].astype(F32) - self.center) * self.scale + self.offset
        value = half + half * jnp.tanh(half)
        inside = None
        for at, extent, index, count in (
            (r, HALO_ROWS, lax.axis_index("ha"), NH),
            (c, HALO_COLS, lax.axis_index("wa"), NX * NZ),
        ):
            if at in (0, extent - 1):
                here = index > 0 if at == 0 else index < count - 1
                inside = here if inside is None else jnp.logical_and(inside, here)
        if inside is not None:
            value = jnp.where(inside, value, 0.0)
        self.act[r, c] = value.astype(BF16)


TAPS = ((1, 1), (0, 1), (2, 1), (1, 0), (1, 2), (0, 0), (0, 2), (2, 0), (2, 2))


def convolve(activation, weight, first, delayed):
    act = activation.act
    channels = act.shape[-1]
    made = set()
    result = first
    for time_off in range(3):
        total = None
        for row_off, col_off in TAPS:
            for r in range(row_off, row_off + ROWS):
                for c in range(col_off, col_off + COLS):
                    if (r, c) not in made:
                        activation.cell(r, c)
                        made.add((r, c))
            window = act[row_off : row_off + ROWS, col_off : col_off + COLS]
            product = jnp.dot(
                window.reshape(LOCAL, channels),
                weight[time_off, row_off, col_off],
                preferred_element_type=F32,
            )
            total = product if total is None else total + product
        total = total.reshape(CELLS, FRAMES, CO)
        late = 2 - time_off
        if late:
            delayed[late - 1, :, 8:, :] = total
            total = delayed[late - 1, :, 8 - late : 8 - late + FRAMES, :]
        result = result + total
    return result


def stage_cache(cache, wide, rows_ref, edge_ref):
    wide[...] = jnp.zeros_like(wide)
    for frame in range(2):
        for c in range(COLS):
            both = cache[frame, c].astype(F32)
            for r in range(ROWS):
                wide[frame, 1 + r, 1 + c : 2 + c, :] = both[r : r + 1]
            if c in (0, COLS - 1):
                edge_ref[min(c, 1), frame * ROWS : frame * ROWS + ROWS, :] = both
        for r in range(ROWS):
            rows_ref[r, frame] = wide[frame, 1 + r, 1:17, :].astype(BF16)


def shift_cache(got_rows, got_edge, wide, shifted):
    row, across = lax.axis_index("ha"), lax.axis_index("wa")
    for frame in range(2):
        for r in range(HALO_ROWS):
            inside = {0: row > 0, HALO_ROWS - 1: row < NH - 1}.get(r)
            if inside is None:
                source, entry = 1, frame * ROWS + r - 1
            else:
                upper = r == 0
                own = got_rows[0 if upper else 1, frame].astype(F32)[0:COLS]
                wide[frame, r, 1 : COLS + 1, :] = jnp.where(inside, own, 0.0)
                source, entry = (2, frame * ROWS + ROWS - 1) if upper else (0, frame * ROWS)
            for slot, at, here in ((0, 0, across > 0), (1, COLS + 1, across < NX * NZ - 1)):
                edge = got_edge[source, slot, entry : entry + 1]
                ok = here if inside is None else jnp.logical_and(here, inside)
                wide[frame, r, at : at + 1, :] = jnp.where(ok, edge, 0.0)
    for k in range(3):
        for frame in range(2):
            for r in range(HALO_ROWS):
                shifted[k, frame, r] = wide[frame, r, k : k + 16, :].astype(BF16)


def convolve_cache(shifted, weight, spill):
    channels = shifted.shape[-1]
    both, later = None, None
    for row_off in range(3):
        for k in range(3):
            two = shifted[k, :, row_off : row_off + ROWS].reshape(2 * ROWS * 16, channels)
            one = shifted[k, 1, row_off : row_off + ROWS].reshape(ROWS * 16, channels)
            a = jnp.dot(two, weight[0, row_off, k], preferred_element_type=F32)
            b = jnp.dot(one, weight[1, row_off, k], preferred_element_type=F32)
            both = a if both is None else both + a
            later = b if later is None else later + b
    half = ROWS * 16
    spill[...] = jnp.zeros_like(spill)
    for q in range(CO // 128):
        lanes = slice(128 * q, 128 * q + 128)
        spill[q, 0:half] = both[0:half, lanes] + later[:, lanes]
        spill[q, half : 2 * half] = both[half:, lanes]


def add_cache(spill, total):
    for r in range(ROWS):
        for c in range(COLS):
            for q in range(CO // 128):
                lanes = slice(128 * q, 128 * q + 128)
                total[r * COLS + c, 0:8, lanes] += spill[
                    q, pl.ds(r * 16 + c, 8, stride=ROWS * 16)
                ]


def kernel(
    features, cache_one, gain_one_in, shift_one_in, weight_one, cache_two, gain_two_in, shift_two_in, weight_two,
    bias_in, skip,
    out,
    gain_one, shift_one, gain_two, shift_two, bias,
    feats, wide_feats, cells_one, act_one, cells_two, act_two, w_one, w_two, w_skip,
    c_one, c_two, rows_one, rows_two, edge_one, edge_two,
    got_rows_one, got_rows_two, got_edge_one, got_edge_two,
    wide_one, wide_two, shifted_one, shifted_two, spill, base_one, base_two, delayed,
    src_1a, src_1b, src_core, got_core, src_two, slots_1a, slots_1b, slots_two, slots_far,
    load, stat_send, stat_recv, halo_send, halo_recv,
):
    first_step = len(STAGES[0]) + 1
    loads = [
        pltpu.make_async_copy(features, feats, load.at[0]),
        pltpu.make_async_copy(cache_one, c_one, load.at[1]),
        pltpu.make_async_copy(cache_two, c_two, load.at[2]),
        pltpu.make_async_copy(skip, w_skip, load.at[3]),
    ]
    loads += [
        pltpu.make_async_copy(weight_one.at[i], w_one.at[i], load.at[4 + i]) for i in range(3)
    ]
    loads += [
        pltpu.make_async_copy(weight_two.at[i], w_two.at[i], load.at[7 + i]) for i in range(3)
    ]
    vectors = ((gain_one_in, gain_one), (shift_one_in, shift_one), (gain_two_in, gain_two),
               (shift_two_in, shift_two), (bias_in, bias))
    loads += [pltpu.make_async_copy(*pair, load.at[10 + n]) for n, pair in enumerate(vectors)]
    loads[0].start()

    barrier = pltpu.get_barrier_semaphore()
    greeted = [partner(offset) for offset in sorted(sum(STAGES, ()), key=lambda offset: -hops(offset))]
    greeted += [neighbour(side) for side in SIDES if side[1] != 0]
    for device in greeted:
        pl.semaphore_signal(barrier, inc=1, device_id=device, device_id_type=MESH)
    for copy in loads[1:]:
        copy.start()

    loads[0].wait()
    for t in range(FRAMES):
        for c in range(COLS):
            at = (t * COLS + c) * ROWS
            both = feats[t, c].astype(F32)
            for q in range(CI // 128):
                wide_feats[q, at : at + ROWS, :] = both[:, 128 * q : 128 * q + 128]
    for r in range(ROWS):
        for c in range(COLS):
            for q in range(CI // 128):
                lanes = slice(128 * q, 128 * q + 128)
                cells_one[1 + r, 1 + c, :, lanes] = wide_feats[
                    q, pl.ds(c * ROWS + r, FRAMES, stride=CELLS)
                ].astype(BF16)
    own = cells_one[1 : 1 + ROWS, 1 : 1 + COLS].reshape(LOCAL, CI)
    local_stats(own.astype(F32), src_1a)
    pl.semaphore_wait(barrier, len(greeted))

    send_stats(STAGES[0], src_1a, slots_1a, stat_send.at[0], stat_recv.at[0])
    halo_one = [halo_copy(cells_one, n, halo_send.at[0], halo_recv.at[0]) for n in range(8)]
    cached_one = [
        cache_copy(rows_one, edge_one, got_rows_one, got_edge_one, n, halo_send.at[1], halo_recv.at[1])
        for n in range(8)
    ]
    cached_two = [
        cache_copy(rows_two, edge_two, got_rows_two, got_edge_two, n, halo_send.at[2], halo_recv.at[2])
        for n in range(8)
    ]
    for copy in halo_one:
        copy.start()
    loads[1].wait()
    loads[2].wait()
    stage_cache(c_one, wide_one, rows_one, edge_one)
    for copy in cached_one:
        copy.start()
    stage_cache(c_two, wide_two, rows_two, edge_two)
    for copy in cached_two:
        copy.start()

    for copy in loads[10:] + loads[3:4]:
        copy.wait()
    own = cells_one[1 : 1 + ROWS, 1 : 1 + COLS].reshape(LOCAL, CI)
    shortcut = jnp.dot(own, w_skip[...], preferred_element_type=F32) + as_row(bias[...])
    base_two[...] = shortcut.reshape(CELLS, FRAMES, CO)

    wait_all(slots_1a, stat_recv.at[0])
    src_1b[0:1], src_1b[1:2] = merge_stats(src_1a, slots_1a, LOCAL * CI // GROUPS)
    send_stats(STAGES[1], src_1b, slots_1b, stat_send.at[1], stat_recv.at[1])

    for copy in cached_one:
        copy.wait_recv()
    for n in (4, 5):
        loads[n].wait()
    shift_cache(got_rows_one, got_edge_one, wide_one, shifted_one)
    convolve_cache(shifted_one, w_one, spill)
    base_one[...] = jnp.zeros_like(base_one)
    add_cache(spill, base_one)

    loads[6].wait()
    delayed[:, :, 0:8, :] = jnp.zeros_like(delayed[:, :, 0:8, :])
    for copy in halo_one:
        copy.wait_recv()
    wait_all(slots_1b, stat_recv.at[1])
    center, spread = merge_stats(src_1b, slots_1b, LOCAL * first_step * CI // GROUPS)
    mean = unpack_groups(center, CI // 128, 0, CI // GROUPS)
    variance = unpack_groups(spread * (GROUPS / (LOCAL * DEVICES * CI)), CI // 128, 0, CI // GROUPS)
    activation = Activation(cells_one, act_one, mean, variance, gain_one[...], shift_one[...])
    middle = convolve(activation, w_one, base_one[...], delayed).astype(BF16)
    cells_two[1 : 1 + ROWS, 1 : 1 + COLS] = middle.reshape(ROWS, COLS, FRAMES, CO)
    halo_two = [halo_copy(cells_two, n, halo_send.at[3], halo_recv.at[3]) for n in range(8)]
    for copy in halo_two:
        copy.start()
    local_stats(middle.astype(F32).reshape(LOCAL, CO), src_core)
    row, across = lax.axis_index("ha"), lax.axis_index("wa")
    swap = pltpu.make_async_remote_copy(
        src_ref=src_core,
        dst_ref=got_core,
        send_sem=stat_send.at[3],
        recv_sem=stat_recv.at[3],
        device_id=(other_core(row), across),
        device_id_type=MESH,
    )
    swap.start()
    send_far(src_core, slots_far, stat_send.at[4], stat_recv.at[4])
    swap.wait()
    src_two[...] = merge_cores(src_core[...], got_core[...], CO // GROUPS)
    send_stats(NEAR, src_two, slots_two, stat_send.at[2], stat_recv.at[2])

    for copy in cached_two:
        copy.wait_recv()
    for n in (7, 8):
        loads[n].wait()
    shift_cache(got_rows_two, got_edge_two, wide_two, shifted_two)
    convolve_cache(shifted_two, w_two, spill)
    add_cache(spill, base_two)

    loads[9].wait()
    for copy in halo_one + cached_one + cached_two + halo_two:
        copy.wait_send()
    wait_all(slots_1a, stat_send.at[0])
    wait_all(slots_1b, stat_send.at[1])
    for copy in halo_two:
        copy.wait_recv()
    wait_all(slots_two, stat_recv.at[2])
    joined = src_two[...]
    near = deviations(joined, slots_two)
    wait_all(slots_far, stat_recv.at[4])
    far = deviations(joined, slots_far)
    mean, variance = merge_direct(joined, near, far, 1 + len(NEAR) + 2 * len(FAR), CO // GROUPS)
    activation = Activation(cells_two, act_two, mean, variance, gain_two[...], shift_two[...])
    decoded = convolve(activation, w_two, base_two[...], delayed)
    out[...] = decoded.reshape(ROWS, COLS, FRAMES, CO).astype(BF16)
    wait_all(slots_two, stat_send.at[2])
    wait_all(slots_far, stat_send.at[4])


def by_column(tile):
    return jnp.transpose(tile, (0, 2, 1, 3))


def on_device(
    features, first_cache, first_gain, first_shift, first_weight,
    second_cache, second_gain, second_shift, second_weight, second_bias, skip_weight,
):
    vmem = pl.BlockSpec(memory_space=pltpu.VMEM)
    hbm = pl.BlockSpec(memory_space=pltpu.HBM)
    cells = (HALO_ROWS, HALO_COLS, FRAMES)

    def per_conv(channels):
        return [
            pltpu.VMEM((2, COLS, ROWS, channels), BF16),
            pltpu.VMEM((ROWS, 2, 16, channels), BF16),
            pltpu.VMEM((2, 2 * ROWS, channels), F32),
            pltpu.VMEM((2, 2, 16, channels), BF16),
            pltpu.VMEM((3, 2, 2 * ROWS, channels), F32),
            pltpu.VMEM((2, HALO_ROWS, 24, channels), F32),
            pltpu.VMEM((3, 2, HALO_ROWS, 16, channels), BF16),
        ]

    one, two = per_conv(CI), per_conv(CO)
    paired = [scratch for pair in zip(one, two) for scratch in pair]
    out = pl.pallas_call(
        kernel,
        out_shape=pltpu.VMEM((ROWS, COLS, FRAMES, CO), BF16),
        in_specs=[hbm] * 11,
        out_specs=vmem,
        scratch_shapes=[
            pltpu.VMEM((CI // 128, 128), F32),
            pltpu.VMEM((CI // 128, 128), F32),
            pltpu.VMEM((CO // 128, 128), F32),
            pltpu.VMEM((CO // 128, 128), F32),
            pltpu.VMEM((CO // 128, 128), F32),
            pltpu.VMEM((FRAMES, COLS, ROWS, CI), BF16),
            pltpu.VMEM((CI // 128, LOCAL, 128), F32),
            pltpu.VMEM(cells + (CI,), BF16),
            pltpu.VMEM(cells + (CI,), BF16),
            pltpu.VMEM(cells + (CO,), BF16),
            pltpu.VMEM(cells + (CO,), BF16),
            pltpu.VMEM((3, 3, 3, CI, CO), BF16),
            pltpu.VMEM((3, 3, 3, CO, CO), BF16),
            pltpu.VMEM((CI, CO), BF16),
            *paired,
            pltpu.VMEM((CO // 128, 8 * ROWS * 16, 128), F32),
            pltpu.VMEM((CELLS, FRAMES, CO), F32),
            pltpu.VMEM((CELLS, FRAMES, CO), F32),
            pltpu.VMEM((2, CELLS, FRAMES + 8, CO), F32),
            pltpu.VMEM((2, 128), F32),
            pltpu.VMEM((2, 128), F32),
            pltpu.VMEM((1, 128), F32),
            pltpu.VMEM((1, 128), F32),
            pltpu.VMEM((1, 128), F32),
            pltpu.VMEM((len(STAGES[0]), 2, 128), F32),
            pltpu.VMEM((len(STAGES[1]), 2, 128), F32),
            pltpu.VMEM((len(NEAR), 1, 128), F32),
            pltpu.VMEM((2 * len(FAR), 1, 128), F32),
            pltpu.SemaphoreType.DMA((15,)),
            pltpu.SemaphoreType.DMA((5,)),
            pltpu.SemaphoreType.DMA((5,)),
            pltpu.SemaphoreType.DMA((4, 8)),
            pltpu.SemaphoreType.DMA((4, 8)),
        ],
        compiler_params=pltpu.CompilerParams(
            collective_id=0, has_side_effects=True, vmem_limit_bytes=63 << 20
        ),
        cost_estimate=pl.CostEstimate(
            flops=2 * LOCAL * CO * (27 * CI + 27 * CO + CI),
            bytes_accessed=2 * (27 * (CI + CO) + CI) * CO + 2 * LOCAL * (CI + CO),
            transcendentals=48 * FRAMES * (CI + CO),
        ),
    )(
        by_column(features),
        by_column(first_cache),
        first_gain.reshape(CI // 128, 128),
        first_shift.reshape(CI // 128, 128),
        first_weight,
        by_column(second_cache),
        second_gain.reshape(CO // 128, 128),
        second_shift.reshape(CO // 128, 128),
        second_weight,
        second_bias.reshape(CO // 128, 128),
        skip_weight,
    )
    return jnp.transpose(out, (2, 0, 1, 3))


def solution(mesh):
    tile = P(None, "ha", "wa", None)
    return jax.shard_map(
        on_device,
        mesh=mesh,
        in_specs=(tile, tile, P(), P(), P(), tile, P(), P(), P(), P(), P()),
        out_specs=tile,
        check_vma=False,
    )
```

```python
import functools

import jax
import jax.numpy as jnp
from jax import lax
from jax.experimental import pallas as pl
from jax.experimental.pallas import tpu as pltpu
from jax.sharding import PartitionSpec as P

F32 = jnp.float32
BF16 = jnp.bfloat16
MESH = pl.DeviceIdType.MESH
EPSILON = 1e-06

FRAMES = 16
ROWS, COLS = 2, 10
HALO_ROWS, HALO_COLS = ROWS + 2, COLS + 2
CELLS = ROWS * COLS
CI, CO = 512, 256
GROUPS = 32
NH, NX, NZ = 8, 4, 8
LOCAL = FRAMES * CELLS
DEVICES = NH * NX * NZ

def hops(offset):
    row, x, z = offset
    return min(row, NH - row) / 2 + min(x, NX - x) + min(z, NZ - z)


STAGES = tuple(
    tuple(sorted(stage, key=lambda offset: -hops(offset)))
    for stage in (
        [(0, 0, c) for c in range(1, NZ)],
        [(a, b, 0) for a in range(NH) for b in range(NX) if (a, b) != (0, 0)],
    )
)
CHIPS = sorted(
    (
        (a, b, c)
        for a in range(0, NH, 2)
        for b in range(NX)
        for c in range(NZ)
        if (a, b, c) != (0, 0, 0)
    ),
    key=lambda offset: -hops(offset),
)
FAR = [offset for offset in CHIPS if hops(offset) >= 6]
NEAR = CHIPS[len(FAR) :]
SIDES = tuple((a, b) for a in (-1, 0, 1) for b in (-1, 0, 1) if (a, b) != (0, 0))


def place():
    across = lax.axis_index("wa")
    return lax.axis_index("ha"), lax.rem(across, NX), lax.div(across, NX)


def partner(offset):
    row, x, z = place()
    return (
        lax.rem(row + offset[0], NH),
        lax.rem(z + offset[2], NZ) * NX + lax.rem(x + offset[1], NX),
    )


def other_core(row):
    return row + 1 - 2 * lax.rem(row, 2)


def neighbour(side):
    row, across = lax.axis_index("ha"), lax.axis_index("wa")
    return lax.rem(row + side[0] + NH, NH), lax.rem(across + side[1] + NX * NZ, NX * NZ)


def span(step, extent):
    if step == 0:
        return pl.ds(1, extent), pl.ds(1, extent)
    if step < 0:
        return pl.ds(1, 1), pl.ds(extent + 1, 1)
    return pl.ds(extent, 1), pl.ds(0, 1)


def halo_copy(ref, number, send, recv):
    side = SIDES[number]
    row_from, row_to = span(side[0], ROWS)
    col_from, col_to = span(side[1], COLS)
    return pltpu.make_async_remote_copy(
        src_ref=ref.at[row_from, col_from],
        dst_ref=ref.at[row_to, col_to],
        send_sem=send.at[number],
        recv_sem=recv.at[number],
        device_id=neighbour(side),
        device_id_type=MESH,
    )


def cache_copy(rows_ref, edge_ref, got_rows, got_edge, number, send, recv):
    down, right = SIDES[number]
    if right == 0:
        src = rows_ref.at[0 if down < 0 else 1]
        dst = got_rows.at[1 if down < 0 else 0]
    else:
        src = edge_ref.at[0 if right < 0 else 1]
        dst = got_edge.at[down + 1, 1 if right < 0 else 0]
    return pltpu.make_async_remote_copy(
        src_ref=src,
        dst_ref=dst,
        send_sem=send.at[number],
        recv_sem=recv.at[number],
        device_id=neighbour(SIDES[number]),
        device_id_type=MESH,
    )


def send_row(src, dst, send, recv, device):
    pltpu.make_async_remote_copy(
        src_ref=src, dst_ref=dst, send_sem=send, recv_sem=recv, device_id=device, device_id_type=MESH
    ).start()


def send_stats(offsets, src, slots, send, recv, begin=0, end=None):
    for number, offset in list(enumerate(offsets))[begin:end]:
        send_row(src, slots.at[number], send, recv, partner(offset))


def send_far(src, slots, send, recv):
    for number, offset in enumerate(FAR):
        row, across = partner(offset)
        send_row(src, slots.at[2 * number], send, recv, (row, across))
        send_row(src, slots.at[2 * number + 1], send, recv, (other_core(row), across))


def wait_all(slots, sem):
    pltpu.make_async_copy(slots, slots, sem).wait()


def merge_stats(src, slots, entries):
    count = slots.shape[0] + 1
    own = src[...]
    others = slots[...]
    total = own + jnp.sum(others, axis=0)
    center = total[0:1] / count
    off = own[0:1] - center
    offs = others[:, 0] - center
    squares = off * off + jnp.sum(offs * offs, axis=0, keepdims=True)
    return center, total[1:2] + entries * squares


def as_tiles(row):
    return jnp.concatenate(
        [row[:, 128 * q : 128 * q + 128] for q in range(row.shape[1] // 128)], axis=0
    )


def as_row(tiles):
    return jnp.concatenate([tiles[q : q + 1] for q in range(tiles.shape[0])], axis=1)


def group_sum(tiles, per_group):
    rows = tiles.shape[0]
    first = lax.div(lax.broadcasted_iota(jnp.int32, (128, 128), 0), per_group)
    second = lax.div(lax.broadcasted_iota(jnp.int32, (128, 128), 1), per_group)
    same = jnp.where(first == second, 1.0, 0.0).astype(BF16)
    if rows < 8:
        tiles = jnp.concatenate([tiles, jnp.zeros((8 - rows, 128), F32)], axis=0)
    high = tiles.astype(BF16).astype(F32)
    rest = tiles - high
    middle = rest.astype(BF16).astype(F32)
    terms = jnp.concatenate([high, middle, rest - middle], axis=0).astype(BF16)
    sums = jnp.dot(terms, same, preferred_element_type=F32)
    return (sums[0:8] + sums[8:16] + sums[16:24])[:rows]


def lane_of(rows, per_group):
    lane = lax.rem(lax.broadcasted_iota(jnp.int32, (rows, 128), 1), per_group)
    return lane == lax.broadcasted_iota(jnp.int32, (rows, 128), 0)


def pack_groups(tiles, per_group):
    mask = lane_of(tiles.shape[0], per_group)
    return jnp.sum(jnp.where(mask, tiles, 0.0), axis=0, keepdims=True)


def spread_lane(rows, lane, per_group):
    at = lax.broadcasted_iota(jnp.int32, rows.shape, 1)
    return jnp.take_along_axis(rows, at - lax.rem(at, per_group) + lane, axis=1)


def unpack_groups(row, count, first, per_group):
    number = lax.broadcasted_iota(jnp.int32, (8, 128), 0)
    number = jnp.where(number < count, number, 0) + first
    return spread_lane(jnp.broadcast_to(row, (8, 128)), number, per_group)[:count]


def merge_cores(src, other, per_group):
    tiles = GROUPS * per_group // 128
    off = other - src
    lane = lax.rem(lax.broadcasted_iota(jnp.int32, (1, 128), 1), per_group)
    squares = pltpu.roll(off * off * (0.5 * LOCAL * per_group), tiles, 1)
    return jnp.where(lane < tiles, src + 0.5 * off, src + other + squares)


def deviations(own, slots):
    off = slots[:, 0] - own
    return jnp.sum(off, axis=0, keepdims=True), jnp.sum(off * off, axis=0, keepdims=True)


def merge_direct(own, near, far, rows, per_group):
    tiles = GROUPS * per_group // 128
    total = 2.0 * near[0] + far[0]
    squares = 2.0 * near[1] + far[1] - total * total * (1.0 / DEVICES)
    mean = unpack_groups(own + total * (1.0 / DEVICES), tiles, 0, per_group)
    spread = unpack_groups(near[0] + far[0] + rows * own, tiles, tiles, per_group)
    spread += (LOCAL * per_group) * unpack_groups(squares, tiles, 0, per_group)
    return mean, spread * (1.0 / (LOCAL * DEVICES * per_group))


def local_stats(cells, src):
    channels = cells.shape[-1]
    per_group = channels // GROUPS
    first = cells[0:1]
    off = cells - first
    total = jnp.sum(off, axis=0, keepdims=True)
    spread = jnp.sum(off * off, axis=0, keepdims=True) - total * total * (1.0 / LOCAL)
    spread = as_tiles(jnp.maximum(spread, 0.0))
    center = as_tiles(first + total * (1.0 / LOCAL))
    tiles = center.shape[0]
    pivot = spread_lane(center, 0, per_group)
    off = center - pivot
    sums = group_sum(jnp.concatenate([off, spread + LOCAL * (off * off)], axis=0), per_group)
    off = sums[:tiles] * (1.0 / per_group)
    mean = pivot + off
    spread = jnp.maximum(sums[tiles:] - (LOCAL * per_group) * (off * off), 0.0)
    if src.shape[0] == 1:
        src[...] = pack_groups(jnp.concatenate([mean, spread], axis=0), per_group)
    else:
        src[0:1] = pack_groups(mean, per_group)
        src[1:2] = pack_groups(spread, per_group)


class Activation:
    def __init__(self, raw, act, mean, variance, gain, shift):
        self.raw, self.act = raw, act
        self.center = as_row(mean)
        self.scale = as_row(lax.rsqrt(variance + EPSILON) * gain * 0.5)
        self.offset = as_row(shift * 0.5)

    def cell(self, r, c):
        half = (self.raw[r, c].astype(F32) - self.center) * self.scale + self.offset
        value = half + half * jnp.tanh(half)
        inside = None
        for at, extent, index, count in (
            (r, HALO_ROWS, lax.axis_index("ha"), NH),
            (c, HALO_COLS, lax.axis_index("wa"), NX * NZ),
        ):
            if at in (0, extent - 1):
                here = index > 0 if at == 0 else index < count - 1
                inside = here if inside is None else jnp.logical_and(inside, here)
        if inside is not None:
            value = jnp.where(inside, value, 0.0)
        self.act[r, c] = value.astype(BF16)


TAPS = ((1, 1), (0, 1), (2, 1), (1, 0), (1, 2), (0, 0), (0, 2), (2, 0), (2, 2))


def convolve(activation, weight, first, delayed):
    act = activation.act
    channels = act.shape[-1]
    made = set()
    result = first
    for time_off in range(3):
        total = None
        for row_off, col_off in TAPS:
            for r in range(row_off, row_off + ROWS):
                for c in range(col_off, col_off + COLS):
                    if (r, c) not in made:
                        activation.cell(r, c)
                        made.add((r, c))
            window = act[row_off : row_off + ROWS, col_off : col_off + COLS]
            product = jnp.dot(
                window.reshape(LOCAL, channels),
                weight[time_off, row_off, col_off],
                preferred_element_type=F32,
            )
            total = product if total is None else total + product
        total = total.reshape(CELLS, FRAMES, CO)
        late = 2 - time_off
        if late:
            delayed[late - 1, :, 8:, :] = total
            total = delayed[late - 1, :, 8 - late : 8 - late + FRAMES, :]
        result = result + total
    return result


def stage_cache(cache, wide, rows_ref, edge_ref):
    wide[...] = jnp.zeros_like(wide)
    for frame in range(2):
        for c in range(COLS):
            both = cache[frame, c].astype(F32)
            for r in range(ROWS):
                wide[frame, 1 + r, 1 + c : 2 + c, :] = both[r : r + 1]
            if c in (0, COLS - 1):
                edge_ref[min(c, 1), frame * ROWS : frame * ROWS + ROWS, :] = both
        for r in range(ROWS):
            rows_ref[r, frame] = wide[frame, 1 + r, 1:17, :].astype(BF16)


def shift_cache(got_rows, got_edge, wide, shifted):
    row, across = lax.axis_index("ha"), lax.axis_index("wa")
    for frame in range(2):
        for r in range(HALO_ROWS):
            inside = {0: row > 0, HALO_ROWS - 1: row < NH - 1}.get(r)
            if inside is None:
                source, entry = 1, frame * ROWS + r - 1
            else:
                upper = r == 0
                own = got_rows[0 if upper else 1, frame].astype(F32)[0:COLS]
                wide[frame, r, 1 : COLS + 1, :] = jnp.where(inside, own, 0.0)
                source, entry = (2, frame * ROWS + ROWS - 1) if upper else (0, frame * ROWS)
            for slot, at, here in ((0, 0, across > 0), (1, COLS + 1, across < NX * NZ - 1)):
                edge = got_edge[source, slot, entry : entry + 1]
                ok = here if inside is None else jnp.logical_and(here, inside)
                wide[frame, r, at : at + 1, :] = jnp.where(ok, edge, 0.0)
    for k in range(3):
        for frame in range(2):
            for r in range(HALO_ROWS):
                shifted[k, frame, r] = wide[frame, r, k : k + 16, :].astype(BF16)


def convolve_cache(shifted, weight, spill):
    channels = shifted.shape[-1]
    both, later = None, None
    for row_off in range(3):
        for k in range(3):
            two = shifted[k, :, row_off : row_off + ROWS].reshape(2 * ROWS * 16, channels)
            one = shifted[k, 1, row_off : row_off + ROWS].reshape(ROWS * 16, channels)
            a = jnp.dot(two, weight[0, row_off, k], preferred_element_type=F32)
            b = jnp.dot(one, weight[1, row_off, k], preferred_element_type=F32)
            both = a if both is None else both + a
            later = b if later is None else later + b
    half = ROWS * 16
    spill[...] = jnp.zeros_like(spill)
    for q in range(CO // 128):
        lanes = slice(128 * q, 128 * q + 128)
        spill[q, 0:half] = both[0:half, lanes] + later[:, lanes]
        spill[q, half : 2 * half] = both[half:, lanes]


def add_cache(spill, total):
    for r in range(ROWS):
        for c in range(COLS):
            for q in range(CO // 128):
                lanes = slice(128 * q, 128 * q + 128)
                total[r * COLS + c, 0:8, lanes] += spill[
                    q, pl.ds(r * 16 + c, 8, stride=ROWS * 16)
                ]


def kernel(
    features, cache_one, gain_one_in, shift_one_in, weight_one, cache_two, gain_two_in, shift_two_in, weight_two,
    bias_in, skip,
    out,
    gain_one, shift_one, gain_two, shift_two, bias,
    feats, wide_feats, cells_one, act_one, cells_two, act_two, w_one, w_two, w_skip,
    c_one, c_two, rows_one, rows_two, edge_one, edge_two,
    got_rows_one, got_rows_two, got_edge_one, got_edge_two,
    wide_one, wide_two, shifted_one, shifted_two, spill, base_one, base_two, delayed,
    src_1a, src_1b, src_core, got_core, src_two, slots_1a, slots_1b, slots_two, slots_far,
    load, stat_send, stat_recv, halo_send, halo_recv,
):
    first_step = len(STAGES[0]) + 1
    loads = [
        pltpu.make_async_copy(features, feats, load.at[0]),
        pltpu.make_async_copy(cache_one, c_one, load.at[1]),
        pltpu.make_async_copy(cache_two, c_two, load.at[2]),
        pltpu.make_async_copy(skip, w_skip, load.at[3]),
    ]
    loads += [
        pltpu.make_async_copy(weight_one.at[i], w_one.at[i], load.at[4 + i]) for i in range(3)
    ]
    loads += [
        pltpu.make_async_copy(weight_two.at[i], w_two.at[i], load.at[7 + i]) for i in range(3)
    ]
    vectors = ((gain_one_in, gain_one), (shift_one_in, shift_one), (gain_two_in, gain_two),
               (shift_two_in, shift_two), (bias_in, bias))
    loads += [pltpu.make_async_copy(*pair, load.at[10 + n]) for n, pair in enumerate(vectors)]
    loads[0].start()

    barrier = pltpu.get_barrier_semaphore()
    greeted = [partner(offset) for offset in sorted(sum(STAGES, ()), key=lambda offset: -hops(offset))]
    greeted += [neighbour(side) for side in SIDES if side[1] != 0]
    for device in greeted:
        pl.semaphore_signal(barrier, inc=1, device_id=device, device_id_type=MESH)
    for copy in loads[1:]:
        copy.start()

    loads[0].wait()
    for t in range(FRAMES):
        for c in range(COLS):
            at = (t * COLS + c) * ROWS
            both = feats[t, c].astype(F32)
            for q in range(CI // 128):
                wide_feats[q, at : at + ROWS, :] = both[:, 128 * q : 128 * q + 128]
    for r in range(ROWS):
        for c in range(COLS):
            for q in range(CI // 128):
                lanes = slice(128 * q, 128 * q + 128)
                cells_one[1 + r, 1 + c, :, lanes] = wide_feats[
                    q, pl.ds(c * ROWS + r, FRAMES, stride=CELLS)
                ].astype(BF16)
    own = cells_one[1 : 1 + ROWS, 1 : 1 + COLS].reshape(LOCAL, CI)
    local_stats(own.astype(F32), src_1a)
    pl.semaphore_wait(barrier, len(greeted))

    send_stats(STAGES[0], src_1a, slots_1a, stat_send.at[0], stat_recv.at[0])
    halo_one = [halo_copy(cells_one, n, halo_send.at[0], halo_recv.at[0]) for n in range(8)]
    cached_one = [
        cache_copy(rows_one, edge_one, got_rows_one, got_edge_one, n, halo_send.at[1], halo_recv.at[1])
        for n in range(8)
    ]
    cached_two = [
        cache_copy(rows_two, edge_two, got_rows_two, got_edge_two, n, halo_send.at[2], halo_recv.at[2])
        for n in range(8)
    ]
    for copy in halo_one:
        copy.start()
    loads[1].wait()
    loads[2].wait()
    stage_cache(c_one, wide_one, rows_one, edge_one)
    for copy in cached_one:
        copy.start()
    stage_cache(c_two, wide_two, rows_two, edge_two)
    for copy in cached_two:
        copy.start()

    for copy in loads[10:] + loads[3:4]:
        copy.wait()
    own = cells_one[1 : 1 + ROWS, 1 : 1 + COLS].reshape(LOCAL, CI)
    shortcut = jnp.dot(own, w_skip[...], preferred_element_type=F32) + as_row(bias[...])
    base_two[...] = shortcut.reshape(CELLS, FRAMES, CO)

    wait_all(slots_1a, stat_recv.at[0])
    src_1b[0:1], src_1b[1:2] = merge_stats(src_1a, slots_1a, LOCAL * CI // GROUPS)
    send_stats(STAGES[1], src_1b, slots_1b, stat_send.at[1], stat_recv.at[1])

    for copy in cached_one:
        copy.wait_recv()
    for n in (4, 5):
        loads[n].wait()
    shift_cache(got_rows_one, got_edge_one, wide_one, shifted_one)
    convolve_cache(shifted_one, w_one, spill)
    base_one[...] = jnp.zeros_like(base_one)
    add_cache(spill, base_one)

    loads[6].wait()
    delayed[:, :, 0:8, :] = jnp.zeros_like(delayed[:, :, 0:8, :])
    for copy in halo_one:
        copy.wait_recv()
    wait_all(slots_1b, stat_recv.at[1])
    center, spread = merge_stats(src_1b, slots_1b, LOCAL * first_step * CI // GROUPS)
    mean = unpack_groups(center, CI // 128, 0, CI // GROUPS)
    variance = unpack_groups(spread * (GROUPS / (LOCAL * DEVICES * CI)), CI // 128, 0, CI // GROUPS)
    activation = Activation(cells_one, act_one, mean, variance, gain_one[...], shift_one[...])
    middle = convolve(activation, w_one, base_one[...], delayed).astype(BF16)
    cells_two[1 : 1 + ROWS, 1 : 1 + COLS] = middle.reshape(ROWS, COLS, FRAMES, CO)
    halo_two = [halo_copy(cells_two, n, halo_send.at[3], halo_recv.at[3]) for n in range(8)]
    for copy in halo_two:
        copy.start()
    local_stats(middle.astype(F32).reshape(LOCAL, CO), src_core)
    row, across = lax.axis_index("ha"), lax.axis_index("wa")
    swap = pltpu.make_async_remote_copy(
        src_ref=src_core,
        dst_ref=got_core,
        send_sem=stat_send.at[3],
        recv_sem=stat_recv.at[3],
        device_id=(other_core(row), across),
        device_id_type=MESH,
    )
    swap.start()
    send_far(src_core, slots_far, stat_send.at[4], stat_recv.at[4])
    swap.wait()
    src_two[...] = merge_cores(src_core[...], got_core[...], CO // GROUPS)
    send_stats(NEAR, src_two, slots_two, stat_send.at[2], stat_recv.at[2])

    for copy in cached_two:
        copy.wait_recv()
    for n in (7, 8):
        loads[n].wait()
    shift_cache(got_rows_two, got_edge_two, wide_two, shifted_two)
    convolve_cache(shifted_two, w_two, spill)
    add_cache(spill, base_two)

    loads[9].wait()
    for copy in halo_one + cached_one + cached_two + halo_two:
        copy.wait_send()
    wait_all(slots_1a, stat_send.at[0])
    wait_all(slots_1b, stat_send.at[1])
    for copy in halo_two:
        copy.wait_recv()
    wait_all(slots_two, stat_recv.at[2])
    joined = src_two[...]
    near = deviations(joined, slots_two)
    wait_all(slots_far, stat_recv.at[4])
    far = deviations(joined, slots_far)
    mean, variance = merge_direct(joined, near, far, 1 + len(NEAR) + 2 * len(FAR), CO // GROUPS)
    activation = Activation(cells_two, act_two, mean, variance, gain_two[...], shift_two[...])
    decoded = convolve(activation, w_two, base_two[...], delayed)
    out[...] = decoded.reshape(ROWS, COLS, FRAMES, CO).astype(BF16)
    wait_all(slots_two, stat_send.at[2])
    wait_all(slots_far, stat_send.at[4])


def by_column(tile):
    return jnp.transpose(tile, (0, 2, 1, 3))


def on_device(
    features, first_cache, first_gain, first_shift, first_weight,
    second_cache, second_gain, second_shift, second_weight, second_bias, skip_weight,
):
    vmem = pl.BlockSpec(memory_space=pltpu.VMEM)
    hbm = pl.BlockSpec(memory_space=pltpu.HBM)
    cells = (HALO_ROWS, HALO_COLS, FRAMES)

    def per_conv(channels):
        return [
            pltpu.VMEM((2, COLS, ROWS, channels), BF16),
            pltpu.VMEM((ROWS, 2, 16, channels), BF16),
            pltpu.VMEM((2, 2 * ROWS, channels), F32),
            pltpu.VMEM((2, 2, 16, channels), BF16),
            pltpu.VMEM((3, 2, 2 * ROWS, channels), F32),
            pltpu.VMEM((2, HALO_ROWS, 24, channels), F32),
            pltpu.VMEM((3, 2, HALO_ROWS, 16, channels), BF16),
        ]

    one, two = per_conv(CI), per_conv(CO)
    paired = [scratch for pair in zip(one, two) for scratch in pair]
    out = pl.pallas_call(
        kernel,
        out_shape=pltpu.VMEM((ROWS, COLS, FRAMES, CO), BF16),
        in_specs=[hbm] * 11,
        out_specs=vmem,
        scratch_shapes=[
            pltpu.VMEM((CI // 128, 128), F32),
            pltpu.VMEM((CI // 128, 128), F32),
            pltpu.VMEM((CO // 128, 128), F32),
            pltpu.VMEM((CO // 128, 128), F32),
            pltpu.VMEM((CO // 128, 128), F32),
            pltpu.VMEM((FRAMES, COLS, ROWS, CI), BF16),
            pltpu.VMEM((CI // 128, LOCAL, 128), F32),
            pltpu.VMEM(cells + (CI,), BF16),
            pltpu.VMEM(cells + (CI,), BF16),
            pltpu.VMEM(cells + (CO,), BF16),
            pltpu.VMEM(cells + (CO,), BF16),
            pltpu.VMEM((3, 3, 3, CI, CO), BF16),
            pltpu.VMEM((3, 3, 3, CO, CO), BF16),
            pltpu.VMEM((CI, CO), BF16),
            *paired,
            pltpu.VMEM((CO // 128, 8 * ROWS * 16, 128), F32),
            pltpu.VMEM((CELLS, FRAMES, CO), F32),
            pltpu.VMEM((CELLS, FRAMES, CO), F32),
            pltpu.VMEM((2, CELLS, FRAMES + 8, CO), F32),
            pltpu.VMEM((2, 128), F32),
            pltpu.VMEM((2, 128), F32),
            pltpu.VMEM((1, 128), F32),
            pltpu.VMEM((1, 128), F32),
            pltpu.VMEM((1, 128), F32),
            pltpu.VMEM((len(STAGES[0]), 2, 128), F32),
            pltpu.VMEM((len(STAGES[1]), 2, 128), F32),
            pltpu.VMEM((len(NEAR), 1, 128), F32),
            pltpu.VMEM((2 * len(FAR), 1, 128), F32),
            pltpu.SemaphoreType.DMA((15,)),
            pltpu.SemaphoreType.DMA((5,)),
            pltpu.SemaphoreType.DMA((5,)),
            pltpu.SemaphoreType.DMA((4, 8)),
            pltpu.SemaphoreType.DMA((4, 8)),
        ],
        compiler_params=pltpu.CompilerParams(
            collective_id=0, has_side_effects=True, vmem_limit_bytes=63 << 20
        ),
        cost_estimate=pl.CostEstimate(
            flops=2 * LOCAL * CO * (27 * CI + 27 * CO + CI),
            bytes_accessed=2 * (27 * (CI + CO) + CI) * CO + 2 * LOCAL * (CI + CO),
            transcendentals=48 * FRAMES * (CI + CO),
        ),
    )(
        by_column(features),
        by_column(first_cache),
        first_gain.reshape(CI // 128, 128),
        first_shift.reshape(CI // 128, 128),
        first_weight,
        by_column(second_cache),
        second_gain.reshape(CO // 128, 128),
        second_shift.reshape(CO // 128, 128),
        second_weight,
        second_bias.reshape(CO // 128, 128),
        skip_weight,
    )
    return jnp.transpose(out, (2, 0, 1, 3))


def solution(mesh):
    tile = P(None, "ha", "wa", None)
    return jax.shard_map(
        on_device,
        mesh=mesh,
        in_specs=(tile, tile, P(), P(), P(), tile, P(), P(), P(), P(), P()),
        out_specs=tile,
        check_vma=False,
    )
```
